128 devices in a mesh: role: 2 (over y_hi), dev: 64 (over z, x, y_lo, core).
Axes of the slice: x: 4, y: 4 (y_hi: 2, y_lo: 2; y = y_hi * 2 + y_lo), z: 4, core: 2. Of those that a mesh axis runs over, the one named last changes fastest.
Arguments:
- tokens: bfloat16 [65536, 1024], P(('role', 'dev')), may hold values from -6 to 6
- expert_ids: int32 [65536, 1], P(('role', 'dev')), may hold values from 0 to 127; in each aligned block of 512 rows (0 to 511, 512 to 1023, ...) at most 8 rows name the same one
- w_qkv: bfloat16 [1024, 3072], P(('role', 'dev')), may hold values from -2 to 2
- w_attn_out: bfloat16 [1024, 1024], P(('role', 'dev')), may hold values from -0.1875 to 0.1875
- gain_attn: bfloat16 [1024], replicated, may hold values from 0.5 to 1.5
- gain_expert: bfloat16 [1024], replicated, may hold values from 0.5 to 1.5
- router: bfloat16 [1024, 128], replicated, may hold values from -0.375 to 0.375
- expert_in: bfloat16 [128, 1024, 2816], P(('role', 'dev')), may hold values from -0.1875 to 0.1875
- expert_out: bfloat16 [128, 2816, 1024], P(('role', 'dev')), may hold values from -0.109375 to 0.109375
- capacity: int32 [128], replicated, may hold values from 256 to 1023
- swap_list: int32 [32], replicated, may hold values from 0 to 63, as said below
Outputs:
- mixed: bfloat16 [65536, 1024], P(('role', 'dev'))
The draws below stay inside these ranges and needn't reach their ends.
Inputs may be any that keep to these rules, and one draw needn't show every extreme that they name: `expert_ids`: in the rows of one device no expert is named more than 8 times, a bound that some block reaches. `swap_list`: entries are distinct.
All inputs are finite; a program needn't handle non-finite values.
Results may differ from the reference program's by a relative error of at most 0.0052.
Values may be sent and summed in bfloat16 or wider, within the bound.
A program may use at most 128 MiB of HBM per device.

```python
import math
import jax
import jax.numpy as jnp
import numpy as np
from jax import lax

D = 1024
HEADS = 16
FF = 2816
TOK_DEV = 512
EXPERTS = 128
C = 8
PAIRS = 32
TOKENS = 65536
N_ROLE = 2
N_DEV = 64


def draw_tokens(key, part):
    keys = jax.random.split(key, 1)
    base = jax.random.normal(keys[0], (TOKENS, D), jnp.float32)
    return jnp.clip(base, -6.0, 6.0).astype(jnp.bfloat16)


def draw_w_qkv(key, part):
    keys = jax.random.split(key, 1)
    base = jax.random.normal(keys[0], (D, 3 * D), jnp.float32) * D ** (-0.5)
    return jnp.clip(base, -2.0, 2.0).astype(jnp.bfloat16)


def draw_swap_list(key, part):
    return jax.random.permutation(key, N_DEV)[:PAIRS].astype(jnp.int32)


def set_ends(array, rng, least, high):
    index_at = [jax.random.randint(jax.random.fold_in(rng, axis), (), 0, length) for axis, length in enumerate(array.shape)]
    main_axis = array.shape.index(max(array.shape))
    next_to = index_at[:main_axis] + [(index_at[main_axis] + 1) % array.shape[main_axis]] + index_at[main_axis + 1:]
    return array.at[tuple(index_at)].set(least).at[tuple(next_to)].set(high)


def levels(stream_key, shape, pieces, smallest, largest):
    level, own = 1.0, jax.random.fold_in(stream_key, 6)
    for dim, blocks in pieces:
        heights = jnp.exp(jax.random.uniform(jax.random.fold_in(own, dim), (blocks,), jnp.float32, smallest / len(pieces), largest / len(pieces)))
        level = level * jnp.repeat(heights, shape[dim] // blocks).reshape([-1 if axis == dim else 1 for axis in range(len(shape))])
    return level


def deal_out(stream_key, own, number, rows, count, top, reach, slope):
    sequence = jax.random.permutation(stream_key, count)
    heavy_load, ordinary = load_shares(count, rows * top, reach, slope, True), load_shares(count, rows * top, reach, slope, False)
    places = jnp.arange(count)

    def named(tallies, rotation):
        used = int((tallies > 0).sum())
        fixed = max(1, used // 4)
        shifted = fixed + (places - fixed + rotation * (used - fixed)) % max(1, count - fixed)
        return jnp.zeros((count,), jnp.int32).at[sequence[jnp.where(places < fixed, places, shifted)]].set(jnp.asarray(tallies, jnp.int32))

    tallies = jnp.where(number % 4 == 0, named(heavy_load, number // 4), named(ordinary, number - number // 4 - 1))
    mixed = jax.random.permutation(jax.random.fold_in(own, 3), count)
    source_of, taker = mixed[0:count // 2 * 2:2], mixed[1:count // 2 * 2:2]
    margin = jnp.minimum(tallies[source_of] - 1, reach - tallies[taker]) // 2
    margin = jnp.where((source_of == sequence[0]) | (taker == sequence[0]) | (tallies[taker] == 0), 0, jnp.maximum(margin, 0))
    shifted = jax.random.randint(jax.random.fold_in(own, 4), (count // 2,), 0, 1 << 20) % (margin + 1)
    tallies = tallies.at[source_of].add(-shifted).at[taker].add(shifted)
    labels = jnp.searchsorted(jnp.cumsum(tallies), jnp.arange(rows * top), side="right").astype(jnp.int32)
    listing = labels.reshape(top, rows).T
    listing = listing[jax.random.permutation(jax.random.fold_in(own, 1), rows)]
    rotation = jax.random.randint(jax.random.fold_in(own, 2), (rows, 1), 0, top)
    return jnp.take_along_axis(listing, (jnp.arange(top)[None, :] + rotation) % top, axis=1)


def load_shares(count, total, most, slope, full):
    weights = [(1 << 20) // math.isqrt(grade ** slope) + 1 for grade in range(1, count + 1)]
    largest = most if full else min(most, max(-(-total // count), total * weights[0] // sum(weights)))
    least = 1 if total - largest >= count - 1 else 0
    holding, rest = [largest] + [least] * (count - 1), total - largest - least * (count - 1)
    while rest > 0:
        movable = [i for i in range(1, count) if holding[i] < largest] or [i for i in range(1, count) if holding[i] < most]
        pool, remaining = sum([weights[i] for i in movable]), rest
        for i in movable:
            more = min(most - holding[i], max(1, remaining * weights[i] // pool), rest)
            holding[i] = holding[i] + more
            rest = rest - more
    return np.array(holding)


def centred(rng, dims, scale, most, cuts=(), kind=jnp.bfloat16):
    gain = levels(rng, dims, cuts, -0.22, 0.18) if cuts else 1.0
    drawn = jax.random.normal(rng, dims, jnp.float32) * scale * gain
    return jnp.minimum(jnp.maximum(drawn, -most), most).astype(kind)


def setup_inputs(seed: int = 0) -> dict:
    streams_of = jax.random.split(jax.random.key(seed), 12)
    tokens = draw_tokens(jax.random.fold_in(streams_of[11], 71), 0)
    expert_ids_keys = jax.random.split(jax.random.fold_in(streams_of[1], 1), TOKENS // TOK_DEV)
    expert_ids_turns = jax.random.permutation(jax.random.fold_in(streams_of[1], 3), TOKENS // TOK_DEV)
    expert_ids = jax.vmap(lambda own, number: deal_out(jax.random.fold_in(streams_of[1], 2), own, number, TOK_DEV, EXPERTS, 1, C, 2))(expert_ids_keys, expert_ids_turns).reshape((TOKENS, 1))
    w_qkv = draw_w_qkv(jax.random.fold_in(streams_of[11], 71), 0)
    w_attn_out = centred(streams_of[3], (D, D), D ** -0.5, 0.1875, ((0, 128),))
    gain_attn = jnp.clip(1.0 + 0.1 * jax.random.normal(streams_of[4], (D,), jnp.float32), 0.5, 1.5).astype(jnp.bfloat16)
    gain_expert = jnp.clip(1.0 + 0.1 * jax.random.normal(streams_of[5], (D,), jnp.float32), 0.5, 1.5).astype(jnp.bfloat16)
    router = centred(streams_of[6], (D, EXPERTS), (D // 4) ** -0.5, 0.375)
    expert_in = centred(streams_of[7], (EXPERTS, D, FF), D ** -0.5, 0.1875, ((0, 128),))
    expert_out = centred(streams_of[8], (EXPERTS, FF, D), FF ** -0.5, 0.109375, ((0, 128),))
    capacity = set_ends(jax.random.randint(streams_of[9], (EXPERTS,), TOK_DEV // 2, 2 * TOK_DEV), jax.random.fold_in(streams_of[9], 1), TOK_DEV // 2, (2 * TOK_DEV) - 1).astype(jnp.int32)
    swap_list = draw_swap_list(jax.random.fold_in(streams_of[11], 71), 0)
    return dict(tokens=tokens, expert_ids=expert_ids, w_qkv=w_qkv, w_attn_out=w_attn_out, gain_attn=gain_attn, gain_expert=gain_expert, router=router, expert_in=expert_in, expert_out=expert_out, capacity=capacity, swap_list=swap_list)


def rms_scale(values, gain_vector):
    mean_sq = lax.optimization_barrier(jnp.mean(values * values, axis=-1, keepdims=True))
    return values * lax.rsqrt(mean_sq + 1e-06) * gain_vector.astype(jnp.float32)

def self_attend(qkv_rows, head_count):
    row_count = qkv_rows.shape[0]
    model_width = qkv_rows.shape[1] // 3
    head_size = model_width // head_count
    queries = qkv_rows[:, :model_width].reshape(row_count, head_count, head_size).astype(jnp.float32)
    keys_all = qkv_rows[:, model_width:2 * model_width].reshape(row_count, head_count, head_size).astype(jnp.float32)
    values = qkv_rows[:, 2 * model_width:].reshape(row_count, head_count, head_size).astype(jnp.float32)
    scores = jnp.einsum('shd,thd->hst', queries, keys_all) * head_size ** (-0.5)
    row_max = lax.optimization_barrier(jnp.max(scores, axis=-1, keepdims=True))
    weights = jnp.exp(scores - row_max)
    soft_weights = (weights / lax.optimization_barrier(jnp.sum(weights, axis=-1, keepdims=True))).astype(jnp.bfloat16)
    context = jnp.einsum('hst,thd->shd', soft_weights.astype(jnp.float32), values)
    return context.reshape(row_count, model_width).astype(jnp.bfloat16)

def reference(tokens, expert_ids, w_qkv, w_attn_out, gain_attn, gain_expert, router, expert_in, expert_out, capacity, swap_list):
    device_count = N_ROLE * N_DEV
    sequences = tokens.reshape(device_count, TOK_DEV, D)

    def one_sequence(block):
        residual = block.astype(jnp.float32)
        normed = rms_scale(residual, gain_attn).astype(jnp.bfloat16)
        qkv_rows = jnp.dot(normed, w_qkv, preferred_element_type=jnp.float32).astype(jnp.bfloat16)
        context = self_attend(qkv_rows, HEADS)
        attended = jnp.dot(context, w_attn_out, preferred_element_type=jnp.float32)
        return residual + attended
    hidden = lax.map(one_sequence, sequences).reshape(device_count * TOK_DEV, D)
    normed_ffn = rms_scale(hidden, gain_expert).astype(jnp.bfloat16)
    logits = jnp.dot(normed_ffn, router, preferred_element_type=jnp.float32)
    chosen = expert_ids[:, 0].astype(jnp.int32)
    gate = jax.nn.sigmoid(jnp.take_along_axis(logits, chosen[:, None], axis=1)[:, 0])
    expert_range = jnp.arange(EXPERTS, dtype=jnp.int32)
    one_hot = (chosen[:, None] == expert_range[None, :]).astype(jnp.int32)
    earlier = jnp.cumsum(one_hot, axis=0) - one_hot
    position = jnp.take_along_axis(earlier, chosen[:, None], axis=1)[:, 0].astype(jnp.int32)
    flagged = jnp.any(swap_list[:, None] == jnp.arange(N_DEV, dtype=jnp.int32)[None, :], axis=0)
    dev_index = expert_range % N_DEV
    role_index = expert_range // N_DEV
    location = jnp.where(flagged[dev_index], (1 - role_index) * N_DEV + dev_index, expert_range).astype(jnp.int32)
    limit = capacity[location][chosen]
    kept = position < limit
    slot_count = EXPERTS * C
    buffer = jnp.zeros((EXPERTS, slot_count, D), jnp.bfloat16).at[chosen, position].set(normed_ffn)

    def one_expert(operands):
        rows_in, weight_in, weight_out = operands
        activ = jnp.maximum(jnp.dot(rows_in, weight_in, preferred_element_type=jnp.float32), 0.0).astype(jnp.bfloat16)
        return jnp.dot(activ, weight_out, preferred_element_type=jnp.float32).astype(jnp.bfloat16)
    results = lax.map(one_expert, (buffer, expert_in, expert_out))
    picked = results[chosen, position].astype(jnp.float32)
    mixed = hidden + jnp.where(kept, gate, jnp.zeros_like(gate))[:, None] * picked
    return mixed.astype(jnp.bfloat16)
```

```python
import jax
import jax.numpy as jnp
from jax import lax
from jax.sharding import PartitionSpec as P

HEADS = 16


def rms_scale(values, gain_vector):
    mean_sq = jnp.mean(values * values, axis=-1, keepdims=True)
    return values * lax.rsqrt(mean_sq + 1e-06) * gain_vector.astype(jnp.float32)


def self_attend(qkv_rows, head_count):
    row_count = qkv_rows.shape[0]
    model_width = qkv_rows.shape[1] // 3
    head_size = model_width // head_count
    queries = qkv_rows[:, :model_width].reshape(row_count, head_count, head_size)
    keys_all = qkv_rows[:, model_width : 2 * model_width].reshape(row_count, head_count, head_size)
    values = qkv_rows[:, 2 * model_width :].reshape(row_count, head_count, head_size)
    scores = jnp.einsum(
        "shd,thd->hst", queries, keys_all, preferred_element_type=jnp.float32
    ) * head_size ** (-0.5)
    row_max = jnp.max(scores, axis=-1, keepdims=True)
    weights = jnp.exp(scores - row_max)
    soft_weights = (weights / jnp.sum(weights, axis=-1, keepdims=True)).astype(jnp.bfloat16)
    context = jnp.einsum("hst,thd->shd", soft_weights, values, preferred_element_type=jnp.float32)
    return context.reshape(row_count, model_width).astype(jnp.bfloat16)


def shards(
    tokens,
    expert_ids,
    w_qkv,
    w_attn_out,
    gain_attn,
    gain_expert,
    router,
    expert_in,
    expert_out,
    capacity,
    swap_list,
):
    seq_len, model_width = tokens.shape
    experts_all = router.shape[1]
    dev_count = lax.axis_size("dev")
    me = lax.axis_index("role") * dev_count + lax.axis_index("dev")
    chosen = expert_ids[:, 0]
    expert_range = jnp.arange(experts_all, dtype=jnp.int32)
    match = chosen[:, None] == expert_range[None, :]
    counts = jnp.sum(match.astype(jnp.float32), axis=0)
    row_share = w_attn_out.shape[0]
    beside = jnp.broadcast_to(counts.astype(jnp.bfloat16)[None, :], (row_share, experts_all))
    w_qkv_all = lax.all_gather(w_qkv, ("role", "dev"), axis=0, tiled=True)
    w_out_counts = lax.all_gather(
        jnp.concatenate([w_attn_out, beside], axis=1), ("role", "dev"), axis=0, tiled=True
    )
    w_out_all = w_out_counts[:, :model_width]
    counts_all = w_out_counts[:, model_width:].astype(jnp.float32)
    residual = tokens.astype(jnp.float32)
    normed = rms_scale(residual, gain_attn).astype(jnp.bfloat16)
    qkv_rows = jnp.dot(normed, w_qkv_all, preferred_element_type=jnp.float32).astype(jnp.bfloat16)
    context = self_attend(qkv_rows, HEADS)
    attended = jnp.dot(context, w_out_all, preferred_element_type=jnp.float32)
    hidden = residual + attended
    normed_ffn = rms_scale(hidden, gain_expert).astype(jnp.bfloat16)
    logits = jnp.dot(normed_ffn, router, preferred_element_type=jnp.float32)
    gate = jax.nn.sigmoid(jnp.sum(jnp.where(match, logits, 0.0), axis=1))
    gathered_row = jnp.arange(w_out_counts.shape[0], dtype=jnp.int32)
    first_of_lower = (gathered_row % row_share == 0) & (gathered_row < me * row_share)
    before = jnp.sum(jnp.where(first_of_lower[:, None], counts_all, 0.0), axis=0).astype(jnp.int32)
    row_ids = lax.broadcasted_iota(jnp.int32, (seq_len, seq_len), 0)
    col_ids = lax.broadcasted_iota(jnp.int32, (seq_len, seq_len), 1)
    strict_lower = (col_ids < row_ids).astype(jnp.bfloat16)
    rank_table = jnp.dot(
        strict_lower, match.astype(jnp.bfloat16), preferred_element_type=jnp.float32
    )
    local_rank = jnp.sum(jnp.where(match, rank_table, 0.0), axis=1).astype(jnp.int32)
    flagged = jnp.any(
        swap_list[:, None] == (expert_range % dev_count)[None, :], axis=0
    )
    location = jnp.where(
        flagged, (1 - expert_range // dev_count) * dev_count + expert_range % dev_count, expert_range
    )
    cap_expert = jnp.sum(
        jnp.where(location[:, None] == expert_range[None, :], capacity[None, :], 0), axis=1
    )
    room = jnp.sum(jnp.where(match, (cap_expert - before)[None, :], 0), axis=1)
    kept = local_rank < room
    slot_rows = max(2, 2 * seq_len // experts_all)
    slot_index = chosen * slot_rows + local_rank
    buffer = (
        jnp.zeros((experts_all * slot_rows, model_width), jnp.bfloat16)
        .at[slot_index]
        .set(normed_ffn)
    )
    buffer = buffer.reshape(experts_all, slot_rows, model_width)
    received = lax.all_to_all(buffer, ("role", "dev"), split_axis=0, concat_axis=0, tiled=True)
    flat_rows = received.reshape(-1, model_width)
    activ = jnp.maximum(
        jnp.dot(flat_rows, expert_in[0], preferred_element_type=jnp.float32), 0.0
    ).astype(jnp.bfloat16)
    produced = jnp.dot(activ, expert_out[0], preferred_element_type=jnp.float32).astype(jnp.bfloat16)
    returned = lax.all_to_all(
        produced.reshape(received.shape), ("role", "dev"), split_axis=0, concat_axis=0, tiled=True
    )
    picked = returned.reshape(-1, model_width)[slot_index].astype(jnp.float32)
    mixed = hidden + jnp.where(kept, gate, 0.0)[:, None] * picked
    return mixed.astype(jnp.bfloat16)


def solution(mesh):
    return jax.shard_map(
        shards,
        mesh=mesh,
        in_specs=(
            P(("role", "dev"), None),
            P(("role", "dev"), None),
            P(("role", "dev"), None),
            P(("role", "dev"), None),
            P(),
            P(),
            P(),
            P(("role", "dev"), None, None),
            P(("role", "dev"), None, None),
            P(),
            P(),
        ),
        out_specs=P(("role", "dev"), None),
        check_vma=False,
    )
```

```python
import jax
import jax.numpy as jnp
from jax import lax
from jax.experimental import pallas as pl
from jax.experimental.pallas import tpu as pltpu
from jax.sharding import PartitionSpec as P

HEADS = 16
MESH = pl.DeviceIdType.MESH

def coordinates():
    role, dev = lax.axis_index("role"), lax.axis_index("dev")
    return {"z": dev // 16, "x": dev // 4 % 4, "y": role * 2 + dev // 2 % 2, "core": dev % 2}

def device_of(at):
    y = at["y"]
    return (y // 2, ((at["z"] * 4 + at["x"]) * 2 + y % 2) * 2 + at["core"])

def moved(at, axis, by):
    size = 2 if axis == "core" else 4
    return {**at, axis: (at[axis] + by) % size}

def block_of(buf, at, whole, cols):
    every = slice(None)
    yh, yl = (every, every) if "y" in whole else (at["y"] // 2, at["y"] % 2)
    z = every if "z" in whole else at["z"]
    x = every if "x" in whole else at["x"]
    return buf.at[yh, z, x, yl, at["core"], every, slice(*cols)]

ORDERS = (("z", "x", "y"), ("x", "y", "z"), ("y", "z", "x"))

class Gather:
    def __init__(self, buf, cols, order, at, send, recv, first):
        self.buf, self.cols, self.order, self.at = buf, cols, order, at
        self.send, self.recv, self.first = send, recv, first
        self.started = []
        span = (cols[1] - cols[0]) // 128
        mid = cols[0] + (span // 2) * 128
        self.halves = ((cols[0], mid), (mid, cols[1]))

    def copy(self, block_at, whole, cols, to, slot):
        ref = block_of(self.buf, block_at, whole, cols)
        return pltpu.make_async_remote_copy(
            src_ref=ref, dst_ref=ref, send_sem=self.send.at[self.first + slot],
            recv_sem=self.recv.at[self.first + slot], device_id=device_of(to), device_id_type=MESH)

    def start(self, *args):
        copy = self.copy(*args)
        copy.start()
        self.started.append(copy)

    def whole(self, phase):
        return self.order[:phase]

    def open_phase(self, phase):
        axis, whole = self.order[phase], self.whole(phase)
        self.start(self.at, whole, self.cols, moved(self.at, axis, 1), phase * 4)
        self.start(self.at, whole, self.cols, moved(self.at, axis, 3), phase * 4 + 1)
        if phase == 2:
            self.start(self.at, whole, self.cols, moved(self.at, "core", 1), 12)

    def turn_phase(self, phase):
        axis, whole = self.order[phase], self.whole(phase)
        left, right = moved(self.at, axis, 3), moved(self.at, axis, 1)
        self.copy(left, whole, self.cols, left, phase * 4).wait_recv()
        self.start(left, whole, self.halves[0], right, phase * 4 + 2)
        self.copy(right, whole, self.cols, right, phase * 4 + 1).wait_recv()
        self.start(right, whole, self.halves[1], left, phase * 4 + 3)
        if phase == 2:
            other = moved(self.at, "core", 1)
            self.start(left, whole, self.cols, other, 13)
            self.start(right, whole, self.cols, other, 14)

    def close_phase(self, phase):
        axis, whole = self.order[phase], self.whole(phase)
        left, right = moved(self.at, axis, 3), moved(self.at, axis, 1)
        far = moved(self.at, axis, 2)
        self.copy(far, whole, self.halves[0], left, phase * 4 + 2).wait_recv()
        self.copy(far, whole, self.halves[1], right, phase * 4 + 3).wait_recv()
        if phase == 2:
            self.start(far, whole, self.cols, moved(self.at, "core", 1), 15)

    def finish(self):
        axis, whole = self.order[2], self.whole(2)
        other = moved(self.at, "core", 1)
        for slot, by in ((12, 0), (13, 3), (14, 1), (15, 2)):
            self.copy(moved(other, axis, by), whole, self.cols, other, slot).wait_recv()

    def drain(self):
        for copy in self.started:
            copy.wait_send()

def greet(at):
    barrier = pltpu.get_barrier_semaphore()
    for axis, by in (("z", 1), ("z", 3), ("x", 1), ("x", 3), ("y", 1), ("y", 3), ("core", 1)):
        pl.semaphore_signal(barrier, inc=1, device_id=device_of(moved(at, axis, by)), device_id_type=MESH)
    pl.semaphore_wait(barrier, 7)

def gather_kernel(qkv_ref, out_ref, qkv_all, out_all, send, recv):
    at = coordinates()
    own = (at["y"] // 2, at["z"], at["x"], at["y"] % 2, at["core"])
    qkv_all[own] = qkv_ref[...]
    out_all[own] = out_ref[...]
    greet(at)
    pieces = []
    for buf, third in ((qkv_all, qkv_ref.shape[1] // 3), (out_all, out_ref.shape[1] // 3)):
        for n, order in enumerate(ORDERS):
            pieces.append(Gather(buf, (n * third, (n + 1) * third), order, at, send, recv, 16 * len(pieces)))
    for phase in range(3):
        for piece in pieces: piece.open_phase(phase)
        for piece in pieces: piece.turn_phase(phase)
        for piece in pieces: piece.close_phase(phase)
    for piece in pieces: piece.finish()
    for piece in pieces: piece.drain()

def gather(w_qkv, w_out):
    lead = (2, 4, 4, 2, 2)
    return pl.pallas_call(
        gather_kernel,
        out_shape=[jax.ShapeDtypeStruct(lead + w_qkv.shape, w_qkv.dtype), jax.ShapeDtypeStruct(lead + w_out.shape, w_out.dtype)],
        in_specs=[pl.BlockSpec(memory_space=pltpu.VMEM)] * 2,
        out_specs=[pl.BlockSpec(memory_space=pltpu.VMEM)] * 2,
        scratch_shapes=[pltpu.SemaphoreType.DMA((96,)), pltpu.SemaphoreType.DMA((96,))],
        compiler_params=pltpu.CompilerParams(collective_id=0, has_side_effects=True, vmem_limit_bytes=40 << 20),
        name="gather_weights",
    )(w_qkv, w_out)


def rms_scale(values, gain_vector):
    mean_sq = jnp.mean(values * values, axis=-1, keepdims=True)
    return values * lax.rsqrt(mean_sq + 1e-06) * gain_vector.astype(jnp.float32)


def self_attend(qkv_rows, head_count):
    row_count = qkv_rows.shape[0]
    model_width = qkv_rows.shape[1] // 3
    head_size = model_width // head_count
    queries = qkv_rows[:, :model_width].reshape(row_count, head_count, head_size)
    keys_all = qkv_rows[:, model_width : 2 * model_width].reshape(row_count, head_count, head_size)
    values = qkv_rows[:, 2 * model_width :].reshape(row_count, head_count, head_size)
    scores = jnp.einsum(
        "shd,thd->hst", queries, keys_all, preferred_element_type=jnp.float32
    ) * head_size ** (-0.5)
    row_max = jnp.max(scores, axis=-1, keepdims=True)
    weights = jnp.exp(scores - row_max)
    soft_weights = (weights / jnp.sum(weights, axis=-1, keepdims=True)).astype(jnp.bfloat16)
    context = jnp.einsum("hst,thd->shd", soft_weights, values, preferred_element_type=jnp.float32)
    return context.reshape(row_count, model_width).astype(jnp.bfloat16)


def shards(
    tokens,
    expert_ids,
    w_qkv,
    w_attn_out,
    gain_attn,
    gain_expert,
    router,
    expert_in,
    expert_out,
    capacity,
    swap_list,
):
    seq_len, model_width = tokens.shape
    experts_all = router.shape[1]
    dev_count = lax.axis_size("dev")
    me = lax.axis_index("role") * dev_count + lax.axis_index("dev")
    chosen = expert_ids[:, 0]
    expert_range = jnp.arange(experts_all, dtype=jnp.int32)
    match = chosen[:, None] == expert_range[None, :]
    counts = jnp.sum(match.astype(jnp.float32), axis=0)
    row_share = w_attn_out.shape[0]
    beside = jnp.broadcast_to(counts.astype(jnp.bfloat16)[None, :], (row_share, experts_all))
    w_qkv_all, w_out_counts = gather(w_qkv, jnp.concatenate([w_attn_out, beside], axis=1))
    w_qkv_all = w_qkv_all.reshape(-1, w_qkv.shape[1])
    w_out_counts = w_out_counts.reshape(w_qkv_all.shape[0], -1)
    w_out_all = w_out_counts[:, :model_width]
    counts_all = w_out_counts[:, model_width:].astype(jnp.float32)
    residual = tokens.astype(jnp.float32)
    normed = rms_scale(residual, gain_attn).astype(jnp.bfloat16)
    qkv_rows = jnp.dot(normed, w_qkv_all, preferred_element_type=jnp.float32).astype(jnp.bfloat16)
    context = self_attend(qkv_rows, HEADS)
    attended = jnp.dot(context, w_out_all, preferred_element_type=jnp.float32)
    hidden = residual + attended
    normed_ffn = rms_scale(hidden, gain_expert).astype(jnp.bfloat16)
    logits = jnp.dot(normed_ffn, router, preferred_element_type=jnp.float32)
    gate = jax.nn.sigmoid(jnp.sum(jnp.where(match, logits, 0.0), axis=1))
    gathered_row = jnp.arange(w_out_counts.shape[0], dtype=jnp.int32)
    first_of_lower = (gathered_row % row_share == 0) & (gathered_row < me * row_share)
    before = jnp.sum(jnp.where(first_of_lower[:, None], counts_all, 0.0), axis=0).astype(jnp.int32)
    row_ids = lax.broadcasted_iota(jnp.int32, (seq_len, seq_len), 0)
    col_ids = lax.broadcasted_iota(jnp.int32, (seq_len, seq_len), 1)
    strict_lower = (col_ids < row_ids).astype(jnp.bfloat16)
    rank_table = jnp.dot(
        strict_lower, match.astype(jnp.bfloat16), preferred_element_type=jnp.float32
    )
    local_rank = jnp.sum(jnp.where(match, rank_table, 0.0), axis=1).astype(jnp.int32)
    flagged = jnp.any(
        swap_list[:, None] == (expert_range % dev_count)[None, :], axis=0
    )
    location = jnp.where(
        flagged, (1 - expert_range // dev_count) * dev_count + expert_range % dev_count, expert_range
    )
    cap_expert = jnp.sum(
        jnp.where(location[:, None] == expert_range[None, :], capacity[None, :], 0), axis=1
    )
    room = jnp.sum(jnp.where(match, (cap_expert - before)[None, :], 0), axis=1)
    kept = local_rank < room
    slot_rows = max(2, 2 * seq_len // experts_all)
    slot_index = chosen * slot_rows + local_rank
    buffer = (
        jnp.zeros((experts_all * slot_rows, model_width), jnp.bfloat16)
        .at[slot_index]
        .set(normed_ffn)
    )
    buffer = buffer.reshape(experts_all, slot_rows, model_width)
    received = lax.all_to_all(buffer, ("role", "dev"), split_axis=0, concat_axis=0, tiled=True)
    flat_rows = received.reshape(-1, model_width)
    activ = jnp.maximum(
        jnp.dot(flat_rows, expert_in[0], preferred_element_type=jnp.float32), 0.0
    ).astype(jnp.bfloat16)
    produced = jnp.dot(activ, expert_out[0], preferred_element_type=jnp.float32).astype(jnp.bfloat16)
    returned = lax.all_to_all(
        produced.reshape(received.shape), ("role", "dev"), split_axis=0, concat_axis=0, tiled=True
    )
    picked = returned.reshape(-1, model_width)[slot_index].astype(jnp.float32)
    mixed = hidden + jnp.where(kept, gate, 0.0)[:, None] * picked
    return mixed.astype(jnp.bfloat16)


def solution(mesh):
    return jax.shard_map(
        shards,
        mesh=mesh,
        in_specs=(
            P(("role", "dev"), None),
            P(("role", "dev"), None),
            P(("role", "dev"), None),
            P(("role", "dev"), None),
            P(),
            P(),
            P(),
            P(("role", "dev"), None, None),
            P(("role", "dev"), None, None),
            P(),
            P(),
        ),
        out_specs=P(("role", "dev"), None),
        check_vma=False,
    )
```

```python
import jax
import jax.numpy as jnp
from jax import lax
from jax.experimental import pallas as pl
from jax.experimental.pallas import tpu as pltpu
from jax.sharding import PartitionSpec as P

HEADS = 16
MESH = pl.DeviceIdType.MESH

def coordinates():
    role, dev = lax.axis_index("role"), lax.axis_index("dev")
    return {"z": dev // 16, "x": dev // 4 % 4, "y": role * 2 + dev // 2 % 2, "core": dev % 2}

def device_of(at):
    y = at["y"]
    return (y // 2, ((at["z"] * 4 + at["x"]) * 2 + y % 2) * 2 + at["core"])

def moved(at, axis, by):
    size = 2 if axis == "core" else 4
    return {**at, axis: (at[axis] + by) % size}

def block_of(buf, at, whole, cols):
    every = slice(None)
    yh, yl = (every, every) if "y" in whole else (at["y"] // 2, at["y"] % 2)
    z = every if "z" in whole else at["z"]
    x = every if "x" in whole else at["x"]
    return buf.at[yh, z, x, yl, at["core"], every, slice(*cols)]

ORDERS = (("z", "x", "y"), ("x", "y", "z"), ("y", "z", "x"))

class Gather:
    def __init__(self, buf, cols, order, at, send, recv, first):
        self.buf, self.cols, self.order, self.at = buf, cols, order, at
        self.send, self.recv, self.first = send, recv, first
        self.started = []
        span = (cols[1] - cols[0]) // 128
        mid = cols[0] + (span // 2) * 128
        self.halves = ((cols[0], mid), (mid, cols[1]))

    def copy(self, block_at, whole, cols, to, slot):
        ref = block_of(self.buf, block_at, whole, cols)
        return pltpu.make_async_remote_copy(
            src_ref=ref, dst_ref=ref, send_sem=self.send.at[self.first + slot],
            recv_sem=self.recv.at[self.first + slot], device_id=device_of(to), device_id_type=MESH)

    def start(self, *args):
        copy = self.copy(*args)
        copy.start()
        self.started.append(copy)

    def whole(self, phase):
        return self.order[:phase]

    def open_phase(self, phase):
        axis, whole = self.order[phase], self.whole(phase)
        self.start(self.at, whole, self.cols, moved(self.at, axis, 1), phase * 4)
        self.start(self.at, whole, self.cols, moved(self.at, axis, 3), phase * 4 + 1)
        if phase == 2:
            self.start(self.at, whole, self.cols, moved(self.at, "core", 1), 12)

    def turn_phase(self, phase):
        axis, whole = self.order[phase], self.whole(phase)
        left, right = moved(self.at, axis, 3), moved(self.at, axis, 1)
        self.copy(left, whole, self.cols, left, phase * 4).wait_recv()
        self.start(left, whole, self.halves[0], right, phase * 4 + 2)
        self.copy(right, whole, self.cols, right, phase * 4 + 1).wait_recv()
        self.start(right, whole, self.halves[1], left, phase * 4 + 3)
        if phase == 2:
            other = moved(self.at, "core", 1)
            self.start(left, whole, self.cols, other, 13)
            self.start(right, whole, self.cols, other, 14)

    def close_phase(self, phase):
        axis, whole = self.order[phase], self.whole(phase)
        left, right = moved(self.at, axis, 3), moved(self.at, axis, 1)
        far = moved(self.at, axis, 2)
        self.copy(far, whole, self.halves[0], left, phase * 4 + 2).wait_recv()
        self.copy(far, whole, self.halves[1], right, phase * 4 + 3).wait_recv()
        if phase == 2:
            self.start(far, whole, self.cols, moved(self.at, "core", 1), 15)

    def finish(self):
        axis, whole = self.order[2], self.whole(2)
        other = moved(self.at, "core", 1)
        for slot, by in ((12, 0), (13, 3), (14, 1), (15, 2)):
            self.copy(moved(other, axis, by), whole, self.cols, other, slot).wait_recv()

    def drain(self):
        for copy in self.started:
            copy.wait_send()

def greet(at):
    barrier = pltpu.get_barrier_semaphore()
    for axis, by in (("z", 1), ("z", 3), ("x", 1), ("x", 3), ("y", 1), ("y", 3), ("core", 1)):
        pl.semaphore_signal(barrier, inc=1, device_id=device_of(moved(at, axis, by)), device_id_type=MESH)
    pl.semaphore_wait(barrier, 7)

def gather_kernel(qkv_ref, out_ref, qkv_all, out_all, send, recv):
    at = coordinates()
    own = (at["y"] // 2, at["z"], at["x"], at["y"] % 2, at["core"])
    qkv_all[own] = qkv_ref[...]
    out_all[own] = out_ref[...]
    greet(at)
    pieces = []
    for buf, third in ((qkv_all, qkv_ref.shape[1] // 3), (out_all, out_ref.shape[1] // 3)):
        for n, order in enumerate(ORDERS):
            pieces.append(Gather(buf, (n * third, (n + 1) * third), order, at, send, recv, 16 * len(pieces)))
    for phase in range(3):
        for piece in pieces: piece.open_phase(phase)
        for piece in pieces: piece.turn_phase(phase)
        for piece in pieces: piece.close_phase(phase)
    for piece in pieces: piece.finish()
    for piece in pieces: piece.drain()

def gather(w_qkv, w_out):
    lead = (2, 4, 4, 2, 2)
    return pl.pallas_call(
        gather_kernel,
        out_shape=[jax.ShapeDtypeStruct(lead + w_qkv.shape, w_qkv.dtype), jax.ShapeDtypeStruct(lead + w_out.shape, w_out.dtype)],
        in_specs=[pl.BlockSpec(memory_space=pltpu.VMEM)] * 2,
        out_specs=[pl.BlockSpec(memory_space=pltpu.VMEM)] * 2,
        scratch_shapes=[pltpu.SemaphoreType.DMA((96,)), pltpu.SemaphoreType.DMA((96,))],
        compiler_params=pltpu.CompilerParams(collective_id=0, has_side_effects=True, vmem_limit_bytes=40 << 20),
        name="gather_weights",
    )(w_qkv, w_out)


STAGES = 4


def shift_of(stage, place):
    dz, dx, dc = place // 8, place // 2 % 4, place % 2
    return dz, dx, (stage + 8 - dz - dx) % 4, dc


def shifted(at, stage, place, sign):
    dz, dx, dy, dc = shift_of(stage, place)
    return {
        "z": (at["z"] + 4 + sign * dz) % 4,
        "x": (at["x"] + 4 + sign * dx) % 4,
        "y": (at["y"] + 4 + sign * dy) % 4,
        "core": (at["core"] + dc) % 2,
    }


def shift_index(at, expert):
    dz = (expert // 16 % 4 - at["z"] + 4) % 4
    dx = (expert // 4 % 4 - at["x"] + 4) % 4
    dy = (expert // 64 * 2 + expert // 2 % 2 - at["y"] + 4) % 4
    dc = (expert - at["core"] + 2) % 2
    return (dz + dx + dy) % 4 * 32 + dz * 8 + dx * 2 + dc


def greet_all(me, count):
    barrier = pltpu.get_barrier_semaphore()

    def greet_one(step, carry):
        peer = (me + step) % count
        pl.semaphore_signal(barrier, inc=1, device_id=(peer // 64, peer % 64), device_id_type=MESH)
        return carry

    lax.fori_loop(1, count, greet_one, 0)
    return barrier


def experts_kernel(
    normed_ref, hidden_ref, slot_row, slot_col, chosen_col, kept_col, router_ref, w_in_hbm, w_out_hbm, mixed_ref,
    sent, held, made, back, w_in, w_out, activ, total, weight_sem, send_sem, recv_sem,
):
    at = coordinates()
    me = lax.axis_index("role") * 64 + lax.axis_index("dev")
    blocks, slot_rows, width = sent.shape
    per = blocks // STAGES
    rows = per * slot_rows
    barrier = greet_all(me, blocks)
    load_in = pltpu.make_async_copy(w_in_hbm.at[0], w_in, weight_sem.at[0])
    load_out = pltpu.make_async_copy(w_out_hbm.at[0], w_out, weight_sem.at[1])
    load_in.start()
    load_out.start()

    def fill(stage):
        wanted = lax.broadcasted_iota(jnp.int32, (rows, slot_row.shape[1]), 0) + stage * rows
        pick = (wanted == slot_row[...]).astype(jnp.bfloat16)
        block = jnp.dot(pick, normed_ref[...], preferred_element_type=jnp.float32).astype(jnp.bfloat16)
        sent[pl.ds(stage * per, per)] = block.reshape(per, slot_rows, width)

    def send_out(stage, place, source, target, way):
        index = stage * per + place
        pltpu.make_async_remote_copy(
            src_ref=source.at[index], dst_ref=target.at[index],
            send_sem=send_sem.at[way], recv_sem=recv_sem.at[way, stage],
            device_id=device_of(shifted(at, stage, place, 1 - 2 * way)), device_id_type=MESH,
        ).start()

    def send_stage(stage, source, target, way):
        first = 1 if stage == 0 else 0

        def one(place, carry):
            send_out(stage, place, source, target, way)
            return carry

        lax.fori_loop(first, per, one, 0)

    def stage_arrived(stage, target, way):
        first = 1 if stage == 0 else 0
        span = pl.ds(stage * per + first, per - first)
        pltpu.make_async_copy(target.at[span], target.at[span], recv_sem.at[way, stage]).wait()

    fill(0)
    pl.semaphore_wait(barrier, blocks - 1)
    held[0] = sent[0]
    send_stage(0, sent, held, 0)
    for stage in range(1, STAGES):
        fill(stage)
        send_stage(stage, sent, held, 0)
    logits = jnp.dot(normed_ref[...], router_ref[...], preferred_element_type=jnp.float32)
    match = lax.broadcasted_iota(jnp.int32, logits.shape, 1) == chosen_col[...]
    gate = jax.nn.sigmoid(jnp.sum(jnp.where(match, logits, 0.0), axis=1, keepdims=True)) * kept_col[...]
    load_in.wait()
    load_out.wait()
    total[...] = jnp.zeros_like(total)

    def take_back(stage):
        stage_arrived(stage, back, 1)
        if stage == 0:
            back[0] = made[0]
        wanted = lax.broadcasted_iota(jnp.int32, (slot_col.shape[0], rows), 1) + stage * rows
        pick = (wanted == slot_col[...]).astype(jnp.bfloat16)
        block = back[pl.ds(stage * per, per)].reshape(rows, width)
        total[...] += jnp.dot(pick, block, preferred_element_type=jnp.float32)

    tile = 256
    for stage in range(STAGES):
        stage_arrived(stage, held, 0)
        block = held[pl.ds(stage * per, per)].reshape(rows, width)
        for t in range(w_in.shape[1] // tile):
            span = slice(t * tile, (t + 1) * tile)
            product = jnp.dot(block, w_in[:, span], preferred_element_type=jnp.float32)
            activ[:, span] = jnp.maximum(product, 0.0).astype(jnp.bfloat16)
        for t in range(width // tile):
            span = slice(t * tile, (t + 1) * tile)
            product = jnp.dot(activ[...], w_out[:, span], preferred_element_type=jnp.float32)
            made[pl.ds(stage * per, per), :, span] = product.astype(jnp.bfloat16).reshape(per, slot_rows, tile)
        send_stage(stage, made, back, 1)
    for stage in range(STAGES):
        take_back(stage)
    mixed_ref[...] = (hidden_ref[...] + gate * total[...]).astype(jnp.bfloat16)
    for way, source in ((0, sent), (1, made)):
        span = pl.ds(1, blocks - 1)
        pltpu.make_async_copy(source.at[span], source.at[span], send_sem.at[way]).wait()


def run_experts(normed, hidden, slot, chosen, kept, router, w_in, w_out):
    tokens, width = normed.shape
    blocks = router.shape[1]
    slot_rows = 2 * tokens // blocks
    exchange = pltpu.VMEM((blocks, slot_rows, width), jnp.bfloat16)
    vmem = pl.BlockSpec(memory_space=pltpu.VMEM)
    hbm = pl.BlockSpec(memory_space=pl.ANY)
    return pl.pallas_call(
        experts_kernel,
        out_shape=jax.ShapeDtypeStruct((tokens, width), jnp.bfloat16),
        in_specs=[vmem] * 7 + [hbm] * 2,
        out_specs=vmem,
        scratch_shapes=[
            exchange, exchange, exchange, exchange,
            pltpu.VMEM(w_in.shape[1:], jnp.bfloat16),
            pltpu.VMEM(w_out.shape[1:], jnp.bfloat16),
            pltpu.VMEM((blocks // STAGES * slot_rows, w_in.shape[2]), jnp.bfloat16),
            pltpu.VMEM((tokens, width), jnp.float32),
            pltpu.SemaphoreType.DMA((2,)),
            pltpu.SemaphoreType.DMA((2,)),
            pltpu.SemaphoreType.DMA((2, STAGES)),
        ],
        compiler_params=pltpu.CompilerParams(collective_id=1, has_side_effects=True, vmem_limit_bytes=56 << 20),
        cost_estimate=pl.CostEstimate(flops=12 * 10**9, bytes_accessed=20 * 2**20, transcendentals=tokens),
        name="experts",
    )(normed, hidden, slot[None, :], slot[:, None], chosen[:, None], kept[:, None], router, w_in, w_out)


def rms_scale(values, gain_vector):
    mean_sq = jnp.mean(values * values, axis=-1, keepdims=True)
    return values * lax.rsqrt(mean_sq + 1e-06) * gain_vector.astype(jnp.float32)


def self_attend(qkv_rows, head_count):
    row_count = qkv_rows.shape[0]
    model_width = qkv_rows.shape[1] // 3
    head_size = model_width // head_count
    queries = qkv_rows[:, :model_width].reshape(row_count, head_count, head_size)
    keys_all = qkv_rows[:, model_width : 2 * model_width].reshape(row_count, head_count, head_size)
    values = qkv_rows[:, 2 * model_width :].reshape(row_count, head_count, head_size)
    scores = jnp.einsum(
        "shd,thd->hst", queries, keys_all, preferred_element_type=jnp.float32
    ) * head_size ** (-0.5)
    row_max = jnp.max(scores, axis=-1, keepdims=True)
    weights = jnp.exp(scores - row_max)
    soft_weights = (weights / jnp.sum(weights, axis=-1, keepdims=True)).astype(jnp.bfloat16)
    context = jnp.einsum("hst,thd->shd", soft_weights, values, preferred_element_type=jnp.float32)
    return context.reshape(row_count, model_width).astype(jnp.bfloat16)


def shards(
    tokens,
    expert_ids,
    w_qkv,
    w_attn_out,
    gain_attn,
    gain_expert,
    router,
    expert_in,
    expert_out,
    capacity,
    swap_list,
):
    seq_len, model_width = tokens.shape
    experts_all = router.shape[1]
    dev_count = lax.axis_size("dev")
    me = lax.axis_index("role") * dev_count + lax.axis_index("dev")
    chosen = expert_ids[:, 0]
    expert_range = jnp.arange(experts_all, dtype=jnp.int32)
    match = chosen[:, None] == expert_range[None, :]
    counts = jnp.sum(match.astype(jnp.float32), axis=0)
    row_share = w_attn_out.shape[0]
    beside = jnp.broadcast_to(counts.astype(jnp.bfloat16)[None, :], (row_share, experts_all))
    w_qkv_all, w_out_counts = gather(w_qkv, jnp.concatenate([w_attn_out, beside], axis=1))
    w_qkv_all = w_qkv_all.reshape(-1, w_qkv.shape[1])
    w_out_counts = w_out_counts.reshape(w_qkv_all.shape[0], -1)
    w_out_all = w_out_counts[:, :model_width]
    counts_all = w_out_counts[:, model_width:].astype(jnp.float32)
    residual = tokens.astype(jnp.float32)
    normed = rms_scale(residual, gain_attn).astype(jnp.bfloat16)
    qkv_rows = jnp.dot(normed, w_qkv_all, preferred_element_type=jnp.float32).astype(jnp.bfloat16)
    context = self_attend(qkv_rows, HEADS)
    attended = jnp.dot(context, w_out_all, preferred_element_type=jnp.float32)
    hidden = residual + attended
    normed_ffn = rms_scale(hidden, gain_expert).astype(jnp.bfloat16)
    gathered_row = jnp.arange(w_out_counts.shape[0], dtype=jnp.int32)
    first_of_lower = (gathered_row % row_share == 0) & (gathered_row < me * row_share)
    before = jnp.sum(jnp.where(first_of_lower[:, None], counts_all, 0.0), axis=0).astype(jnp.int32)
    row_ids = lax.broadcasted_iota(jnp.int32, (seq_len, seq_len), 0)
    col_ids = lax.broadcasted_iota(jnp.int32, (seq_len, seq_len), 1)
    strict_lower = (col_ids < row_ids).astype(jnp.bfloat16)
    rank_table = jnp.dot(
        strict_lower, match.astype(jnp.bfloat16), preferred_element_type=jnp.float32
    )
    local_rank = jnp.sum(jnp.where(match, rank_table, 0.0), axis=1).astype(jnp.int32)
    flagged = jnp.any(
        swap_list[:, None] == (expert_range % dev_count)[None, :], axis=0
    )
    location = jnp.where(
        flagged, (1 - expert_range // dev_count) * dev_count + expert_range % dev_count, expert_range
    )
    cap_expert = jnp.sum(
        jnp.where(location[:, None] == expert_range[None, :], capacity[None, :], 0), axis=1
    )
    room = jnp.sum(jnp.where(match, (cap_expert - before)[None, :], 0), axis=1)
    kept = (local_rank < room).astype(jnp.float32)
    slot_rows = 2 * seq_len // experts_all
    slot = shift_index(coordinates(), chosen) * slot_rows + local_rank
    return run_experts(normed_ffn, hidden, slot, chosen, kept, router, expert_in, expert_out)


def solution(mesh):
    return jax.shard_map(
        shards,
        mesh=mesh,
        in_specs=(
            P(("role", "dev"), None),
            P(("role", "dev"), None),
            P(("role", "dev"), None),
            P(("role", "dev"), None),
            P(),
            P(),
            P(),
            P(("role", "dev"), None, None),
            P(("role", "dev"), None, None),
            P(),
            P(),
        ),
        out_specs=P(("role", "dev"), None),
        check_vma=False,
    )
```

```python
import jax
import jax.numpy as jnp
from jax import lax
from jax.experimental import pallas as pl
from jax.experimental.pallas import tpu as pltpu
from jax.sharding import PartitionSpec as P

HEADS = 16
MESH = pl.DeviceIdType.MESH
GROUPS = 4
STAGES = 4
ORDERS = (("z", "x", "y"), ("x", "y", "z"), ("y", "z", "x"))


def coordinates():
    role, dev = lax.axis_index("role"), lax.axis_index("dev")
    return {"z": dev // 16, "x": dev // 4 % 4, "y": role * 2 + dev // 2 % 2, "core": dev % 2}


def device_of(at):
    y = at["y"]
    return (y // 2, ((at["z"] * 4 + at["x"]) * 2 + y % 2) * 2 + at["core"])


def moved(at, axis, by):
    size = 2 if axis == "core" else 4
    return {**at, axis: (at[axis] + by) % size}


def block_of(buf, at, whole, cols):
    every = slice(None)
    yh, yl = (every, every) if "y" in whole else (at["y"] // 2, at["y"] % 2)
    z = every if "z" in whole else at["z"]
    x = every if "x" in whole else at["x"]
    return buf.at[yh, z, x, yl, at["core"], every, slice(*cols)]


def shift_of(stage, place):
    dz, dx, dc = place // 8, place // 2 % 4, place % 2
    return dz, dx, (stage + 8 - dz - dx) % 4, dc


def shifted(at, stage, place, sign):
    dz, dx, dy, dc = shift_of(stage, place)
    return {
        "z": (at["z"] + 4 + sign * dz) % 4,
        "x": (at["x"] + 4 + sign * dx) % 4,
        "y": (at["y"] + 4 + sign * dy) % 4,
        "core": (at["core"] + dc) % 2,
    }


def shift_index(at, expert):
    dz = ((expert >> 4) - at["z"] + 4) & 3
    dx = ((expert >> 2) - at["x"] + 4) & 3
    dy = ((expert >> 6) * 2 + ((expert >> 1) & 1) - at["y"] + 4) & 3
    dc = (expert - at["core"] + 2) & 1
    return ((dz + dx + dy) & 3) * 32 + dz * 8 + dx * 2 + dc


class Piece:
    def __init__(self, buf, cols, order, at, send, recv, first):
        self.buf, self.cols, self.order, self.at = buf, cols, order, at
        self.send, self.recv, self.first = send, recv, first
        self.started = []

    def copy(self, block_at, whole, to, slot):
        ref = block_of(self.buf, block_at, whole, self.cols)
        return pltpu.make_async_remote_copy(
            src_ref=ref,
            dst_ref=ref,
            send_sem=self.send.at[self.first + slot],
            recv_sem=self.recv.at[self.first + slot],
            device_id=device_of(to),
            device_id_type=MESH,
        )

    def start(self, *args):
        copy = self.copy(*args)
        copy.start()
        self.started.append(copy)

    def open(self, phase):
        axis, whole = self.order[phase], self.order[:phase]
        for by in (1, 3, 2):
            self.start(self.at, whole, moved(self.at, axis, by), phase * 3 + by - 1)

    def arrive(self, phase):
        axis, whole = self.order[phase], self.order[:phase]
        for by in (1, 3, 2):
            source = moved(self.at, axis, -by % 4)
            self.copy(source, whole, source, phase * 3 + by - 1).wait_recv()

    def hand_over(self):
        self.start(self.at, self.order, moved(self.at, "core", 1), 9)

    def taken_over(self):
        other = moved(self.at, "core", 1)
        self.copy(other, self.order, other, 9).wait_recv()

    def drain(self):
        for copy in self.started:
            copy.wait_send()


def greet(at):
    barrier = pltpu.get_barrier_semaphore()
    near = [(axis, by) for axis in ("z", "x", "y") for by in (1, 2, 3)] + [("core", 1)]
    for axis, by in near:
        pl.semaphore_signal(
            barrier, inc=1, device_id=device_of(moved(at, axis, by)), device_id_type=MESH
        )
    return barrier, len(near)


def rms_scale(values, gain):
    mean_sq = jnp.mean(values * values, axis=-1, keepdims=True)
    return values * lax.rsqrt(mean_sq + 1e-06) * gain


def layer_kernel(
    swap_ref, tokens_ref, chosen_ref, qkv_ref, out_ref, gains_ref, router_ref,
    capacity_ref, w_in_hbm, w_out_hbm, mixed_ref,
    qkv_all, out_all, normed, queries, keys, values, summed, context, hidden,
    sent, held, made, back, w_in, w_out, activ, total,
    weight_sem, gather_send, gather_recv, send_sem, recv_sem,
):
    at = coordinates()
    me = lax.axis_index("role") * 64 + lax.axis_index("dev")
    seq_len, width = tokens_ref.shape
    experts_all = router_ref.shape[1]
    barrier, greeted = greet(at)
    load_in = pltpu.make_async_copy(w_in_hbm.at[0], w_in, weight_sem.at[0])
    load_out = pltpu.make_async_copy(w_out_hbm.at[0], w_out, weight_sem.at[1])
    load_in.start()
    load_out.start()

    own = (at["y"] // 2, at["z"], at["x"], at["y"] % 2, at["core"])
    chosen = chosen_ref[...]
    match_t = (
        lax.broadcasted_iota(jnp.int32, (experts_all, seq_len), 0) == chosen
    ).astype(jnp.float32)
    match = match_t.T
    match_low = match.astype(jnp.bfloat16)
    qkv_all[own] = qkv_ref[...]
    share = out_ref.shape[0]
    counts = jnp.dot(
        jnp.ones((share, seq_len), jnp.bfloat16), match_low, preferred_element_type=jnp.float32
    )
    out_all[own] = jnp.concatenate([out_ref[...], counts.astype(jnp.bfloat16)], axis=1)

    chunks, made_pieces = [], 0
    heads_wide = width // GROUPS
    beside = width + experts_all
    spans = [(qkv_all, g * heads_wide, heads_wide, width) for g in range(GROUPS)]
    spans.append((out_all, 0, beside // 3, beside // 3))
    for buf, first, wide, stride in spans:
        chunk = []
        for n, order in enumerate(ORDERS):
            cols = (first + n * stride, first + n * stride + wide)
            chunk.append(Piece(buf, cols, order, at, gather_send, gather_recv, 10 * made_pieces))
            made_pieces += 1
        chunks.append(chunk)

    pl.semaphore_wait(barrier, greeted)
    for chunk in chunks:
        for piece in chunk:
            piece.open(0)
    normed[...] = rms_scale(tokens_ref[...].astype(jnp.float32), gains_ref[0:1]).astype(
        jnp.bfloat16
    )
    for phase in (0, 1):
        for chunk in chunks:
            for piece in chunk:
                piece.arrive(phase)
                piece.open(phase + 1)

    row_ids = lax.broadcasted_iota(jnp.int32, (seq_len, seq_len), 0)
    col_ids = lax.broadcasted_iota(jnp.int32, (seq_len, seq_len), 1)
    lower = (col_ids < row_ids).astype(jnp.bfloat16)
    upper = (row_ids < col_ids).astype(jnp.bfloat16)
    rank_t = jnp.dot(match_t.astype(jnp.bfloat16), upper, preferred_element_type=jnp.float32)
    rank = jnp.dot(lower, match_low, preferred_element_type=jnp.float32)
    rank_col = jnp.sum(match * rank, axis=1, keepdims=True)
    slot_rows = sent.shape[1]
    first_t = shift_index(
        at, lax.broadcasted_iota(jnp.int32, (experts_all, seq_len), 0)
    ).astype(jnp.float32) * slot_rows
    first_row = shift_index(
        at, lax.broadcasted_iota(jnp.int32, (1, experts_all), 1)
    ).astype(jnp.float32) * slot_rows
    slot_row = jnp.sum(match_t * (rank_t + first_t), axis=0, keepdims=True).astype(jnp.int32)
    slot_col = jnp.sum(match * (rank + first_row), axis=1, keepdims=True).astype(jnp.int32)

    def hand_over(chunk):
        for piece in chunk:
            piece.arrive(2)
            piece.hand_over()

    def head_step(head, carry):
        lane = lax.broadcasted_iota(jnp.int32, (1, heads_wide), 1)
        size = width // HEADS
        here = jnp.where((lane // size) == head, 1.0, 0.0).astype(jnp.bfloat16)
        value = values[...] * here
        for half in range(2):
            rows = slice(half * seq_len // 2, (half + 1) * seq_len // 2)
            scores = lax.dot_general(
                queries[rows, :] * here, keys[...], (((1,), (1,)), ((), ())),
                preferred_element_type=jnp.float32,
            )
            weights = jnp.exp(scores - jnp.max(scores, axis=1, keepdims=True))
            norm = 1.0 / jnp.sum(weights, axis=1, keepdims=True)
            part = jnp.dot(weights.astype(jnp.bfloat16), value, preferred_element_type=jnp.float32)
            summed[rows, :] += part * norm
        return carry

    hand_over(chunks[0])
    per_group = HEADS // GROUPS
    scale = (width // HEADS) ** -0.5
    for g in range(GROUPS):
        for piece in chunks[g]:
            piece.taken_over()
        for n, target in enumerate((queries, keys, values)):
            first = n * width + g * heads_wide
            weight = qkv_all[:, :, :, :, :, :, first : first + heads_wide].reshape(width, heads_wide)
            product = jnp.dot(normed[...], weight, preferred_element_type=jnp.float32)
            product = product.astype(jnp.bfloat16)
            target[...] = product * jnp.bfloat16(scale) if n == 0 else product
        summed[...] = jnp.zeros_like(summed)
        lax.fori_loop(0, per_group // 2, head_step, 0)
        hand_over(chunks[g + 1])
        lax.fori_loop(per_group // 2, per_group, head_step, 0)
        context[:, g * heads_wide : (g + 1) * heads_wide] = summed[...].astype(jnp.bfloat16)

    for piece in chunks[GROUPS]:
        piece.taken_over()
    for g in range(GROUPS):
        span = slice(g * heads_wide, (g + 1) * heads_wide)
        weight = out_all[:, :, :, :, :, :, span].reshape(width, heads_wide)
        product = jnp.dot(context[...], weight, preferred_element_type=jnp.float32)
        hidden[:, span] = tokens_ref[:, span].astype(jnp.float32) + product
    normed[...] = rms_scale(hidden[...], gains_ref[1:2]).astype(jnp.bfloat16)

    blocks = sent.shape[0]
    per = blocks // STAGES
    rows = per * slot_rows

    def fill(stage):
        wanted = lax.broadcasted_iota(jnp.int32, (rows, seq_len), 0) + stage * rows
        pick = (wanted == slot_row).astype(jnp.bfloat16)
        block = jnp.dot(pick, normed[...], preferred_element_type=jnp.float32).astype(jnp.bfloat16)
        sent[pl.ds(stage * per, per)] = block.reshape(per, slot_rows, width)

    def send_stage(stage, source, target, way):
        def one(place, carry):
            index = stage * per + place
            pltpu.make_async_remote_copy(
                src_ref=source.at[index],
                dst_ref=target.at[index],
                send_sem=send_sem.at[way],
                recv_sem=recv_sem.at[way, stage],
                device_id=device_of(shifted(at, stage, place, 1 - 2 * way)),
                device_id_type=MESH,
            ).start()
            return carry

        lax.fori_loop(1 if stage == 0 else 0, per, one, 0)

    def stage_arrived(stage, target, way):
        first = 1 if stage == 0 else 0
        span = pl.ds(stage * per + first, per - first)
        pltpu.make_async_copy(target.at[span], target.at[span], recv_sem.at[way, stage]).wait()

    for stage in range(STAGES):
        fill(stage)
        if stage == 0:
            held[0] = sent[0]
        send_stage(stage, sent, held, 0)

    counts_all = out_all[:, :, :, :, :, :, width:beside].reshape(width, experts_all)
    row_of = lax.broadcasted_iota(jnp.int32, (8, width), 1)
    lower_rows = ((row_of % share == 0) & (row_of < me * share)).astype(jnp.bfloat16)
    before = jnp.dot(lower_rows, counts_all, preferred_element_type=jnp.float32)[0:1]
    dev_of = lax.broadcasted_iota(jnp.int32, (1, experts_all), 1) % (experts_all // 2)
    flagged = jnp.zeros((1, experts_all), jnp.int32)
    for n in range(swap_ref.shape[0]):
        flagged = jnp.maximum(flagged, (dev_of == swap_ref[n]).astype(jnp.int32))
    capacity = capacity_ref[...]
    half = experts_all // 2
    traded = jnp.concatenate([capacity[:, half:], capacity[:, :half]], axis=1)
    room = jnp.where(flagged > 0, traded, capacity).astype(jnp.float32) - before
    kept = rank_col < jnp.sum(match * room, axis=1, keepdims=True)
    logits = jnp.dot(normed[...], router_ref[...], preferred_element_type=jnp.float32)
    gate = jax.nn.sigmoid(jnp.sum(match * logits, axis=1, keepdims=True))
    gate = jnp.where(kept, gate, 0.0)
    load_in.wait()
    load_out.wait()
    total[...] = jnp.zeros_like(total)

    tile = 256
    for stage in range(STAGES):
        stage_arrived(stage, held, 0)
        block = held[pl.ds(stage * per, per)].reshape(rows, width)
        for t in range(w_in.shape[1] // tile):
            span = slice(t * tile, (t + 1) * tile)
            product = jnp.dot(block, w_in[:, span], preferred_element_type=jnp.float32)
            activ[:, span] = jnp.maximum(product, 0.0).astype(jnp.bfloat16)
        for t in range(width // tile):
            span = slice(t * tile, (t + 1) * tile)
            product = jnp.dot(activ[...], w_out[:, span], preferred_element_type=jnp.float32)
            made[pl.ds(stage * per, per), :, span] = product.astype(jnp.bfloat16).reshape(
                per, slot_rows, tile
            )
        send_stage(stage, made, back, 1)
    for stage in range(STAGES):
        stage_arrived(stage, back, 1)
        if stage == 0:
            back[0] = made[0]
        wanted = lax.broadcasted_iota(jnp.int32, (seq_len, rows), 1) + stage * rows
        pick = (wanted == slot_col).astype(jnp.bfloat16)
        block = back[pl.ds(stage * per, per)].reshape(rows, width)
        total[...] += jnp.dot(pick, block, preferred_element_type=jnp.float32)
    mixed_ref[...] = (hidden[...] + gate * total[...]).astype(jnp.bfloat16)
    for way, source in ((0, sent), (1, made)):
        span = pl.ds(1, blocks - 1)
        pltpu.make_async_copy(source.at[span], source.at[span], send_sem.at[way]).wait()
    for chunk in chunks:
        for piece in chunk:
            piece.drain()


def shards(
    tokens,
    expert_ids,
    w_qkv,
    w_attn_out,
    gain_attn,
    gain_expert,
    router,
    expert_in,
    expert_out,
    capacity,
    swap_list,
):
    seq_len, width = tokens.shape
    experts_all = router.shape[1]
    slot_rows = 2 * seq_len // experts_all
    lead = (2, 4, 4, 2, 2)
    low, wide = jnp.bfloat16, width // GROUPS
    exchange = pltpu.VMEM((experts_all, slot_rows, width), low)
    vmem = pl.BlockSpec(memory_space=pltpu.VMEM)
    hbm = pl.BlockSpec(memory_space=pl.ANY)
    copies = 10 * 3 * (GROUPS + 1)
    return pl.pallas_call(
        layer_kernel,
        out_shape=jax.ShapeDtypeStruct((seq_len, width), low),
        in_specs=[pl.BlockSpec(memory_space=pltpu.SMEM)] + [vmem] * 7 + [hbm] * 2,
        out_specs=vmem,
        scratch_shapes=[
            pltpu.VMEM(lead + w_qkv.shape, low),
            pltpu.VMEM(lead + (w_attn_out.shape[0], width + experts_all), low),
            pltpu.VMEM((seq_len, width), low),
            pltpu.VMEM((seq_len, wide), low),
            pltpu.VMEM((seq_len, wide), low),
            pltpu.VMEM((seq_len, wide), low),
            pltpu.VMEM((seq_len, wide), jnp.float32),
            pltpu.VMEM((seq_len, width), low),
            pltpu.VMEM((seq_len, width), jnp.float32),
            exchange,
            exchange,
            exchange,
            exchange,
            pltpu.VMEM(expert_in.shape[1:], low),
            pltpu.VMEM(expert_out.shape[1:], low),
            pltpu.VMEM((experts_all // STAGES * slot_rows, expert_in.shape[2]), low),
            pltpu.VMEM((seq_len, width), jnp.float32),
            pltpu.SemaphoreType.DMA((2,)),
            pltpu.SemaphoreType.DMA((copies,)),
            pltpu.SemaphoreType.DMA((copies,)),
            pltpu.SemaphoreType.DMA((2,)),
            pltpu.SemaphoreType.DMA((2, STAGES)),
        ],
        compiler_params=pltpu.CompilerParams(
            collective_id=0, has_side_effects=True, vmem_limit_bytes=58 << 20
        ),
        name="encoder_layer",
    )(
        swap_list, tokens, expert_ids.reshape(1, seq_len), w_qkv, w_attn_out,
        jnp.stack([gain_attn, gain_expert]).astype(jnp.float32), router, capacity[None, :], expert_in, expert_out,
    )


def solution(mesh):
    return jax.shard_map(
        shards,
        mesh=mesh,
        in_specs=(
            P(("role", "dev"), None),
            P(("role", "dev"), None),
            P(("role", "dev"), None),
            P(("role", "dev"), None),
            P(),
            P(),
            P(),
            P(("role", "dev"), None, None),
            P(("role", "dev"), None, None),
            P(),
            P(),
        ),
        out_specs=P(("role", "dev"), None),
        check_vma=False,
    )
```

```python
import jax
import jax.numpy as jnp
from jax import lax
from jax.experimental import pallas as pl
from jax.experimental.pallas import tpu as pltpu
from jax.sharding import PartitionSpec as P

HEADS = 16
MESH = pl.DeviceIdType.MESH
GROUPS = 4
STAGES = 4
ORDERS = (("z", "x", "y"), ("x", "y", "z"), ("y", "z", "x"))


def coordinates():
    role, dev = lax.axis_index("role"), lax.axis_index("dev")
    return {"z": dev // 16, "x": dev // 4 % 4, "y": role * 2 + dev // 2 % 2, "core": dev % 2}


def device_of(at):
    y = at["y"]
    return (y // 2, ((at["z"] * 4 + at["x"]) * 2 + y % 2) * 2 + at["core"])


def moved(at, axis, by):
    size = 2 if axis == "core" else 4
    return {**at, axis: (at[axis] + by) % size}


def block_of(buf, at, whole, cols):
    every = slice(None)
    yh, yl = (every, every) if "y" in whole else (at["y"] // 2, at["y"] % 2)
    z = every if "z" in whole else at["z"]
    x = every if "x" in whole else at["x"]
    return buf.at[yh, z, x, yl, at["core"], every, slice(*cols)]


TWICE = (0, 2, 3, 1)
THRICE = (0, 3, 1, 2)


def crossed(two_bits, mask):
    return (two_bits, two_bits + 1 - 2 * (two_bits % 2), (two_bits + 2) % 4, 3 - two_bits)[mask]


def shifted(at, stage, turn, step, dc, sign):
    dx = crossed(turn, TWICE[step])
    dy = crossed(stage, THRICE[step])
    return {
        "z": (at["z"] + 4 + sign * step) % 4,
        "x": (at["x"] + 4 + sign * dx) % 4,
        "y": (at["y"] + 4 + sign * dy) % 4,
        "core": (at["core"] + dc) % 2,
    }


def shift_index(at, expert):
    dz = ((expert >> 4) - at["z"] + 4) & 3
    dx = ((expert >> 2) - at["x"] + 4) & 3
    dy = ((expert >> 6) * 2 + ((expert >> 1) & 1) - at["y"] + 4) & 3
    dc = (expert - at["core"] + 2) & 1
    twice = ((dz >> 1) ^ (dz & 1)) * 2 + (dz >> 1)
    turn, stage = dx ^ twice, dy ^ twice ^ dz
    return stage * 32 + turn * 8 + dz * 2 + dc


class Piece:
    def __init__(self, buf, cols, order, at, send, recv, first):
        self.buf, self.cols, self.order, self.at = buf, cols, order, at
        self.send, self.recv, self.first = send, recv, first
        self.started = []

    def copy(self, block_at, whole, to, slot):
        ref = block_of(self.buf, block_at, whole, self.cols)
        return pltpu.make_async_remote_copy(
            src_ref=ref,
            dst_ref=ref,
            send_sem=self.send.at[self.first + slot],
            recv_sem=self.recv.at[self.first + slot],
            device_id=device_of(to),
            device_id_type=MESH,
        )

    def start(self, *args):
        copy = self.copy(*args)
        copy.start()
        self.started.append(copy)

    def open(self, phase):
        axis, whole = self.order[phase], self.order[:phase]
        for by in (1, 3, 2):
            self.start(self.at, whole, moved(self.at, axis, by), phase * 3 + by - 1)

    def arrive(self, phase):
        axis, whole = self.order[phase], self.order[:phase]
        for by in (1, 3, 2):
            source = moved(self.at, axis, -by % 4)
            self.copy(source, whole, source, phase * 3 + by - 1).wait_recv()

    def hand_over(self):
        self.start(self.at, self.order, moved(self.at, "core", 1), 9)

    def taken_over(self):
        other = moved(self.at, "core", 1)
        self.copy(other, self.order, other, 9).wait_recv()

    def drain(self):
        for copy in self.started:
            copy.wait_send()


def greet(at):
    barrier = pltpu.get_barrier_semaphore()
    near = [(axis, by) for axis in ("z", "x", "y") for by in (1, 2, 3)] + [("core", 1)]
    for axis, by in near:
        pl.semaphore_signal(
            barrier, inc=1, device_id=device_of(moved(at, axis, by)), device_id_type=MESH
        )
    return barrier, len(near)


def rms_scale(values, gain):
    mean_sq = jnp.mean(values * values, axis=-1, keepdims=True)
    return values * lax.rsqrt(mean_sq + 1e-06) * gain


def layer_kernel(
    swap_ref, tokens_ref, chosen_ref, qkv_ref, out_ref, gains_ref, router_ref,
    capacity_ref, w_in_hbm, w_out_hbm, mixed_ref,
    qkv_all, out_all, normed, queries, keys, values, summed, context, hidden,
    sent, held, made, back, w_in, w_out, activ, total,
    weight_sem, gather_send, gather_recv, send_sem, recv_sem,
):
    at = coordinates()
    me = lax.axis_index("role") * 64 + lax.axis_index("dev")
    seq_len, width = tokens_ref.shape
    experts_all = router_ref.shape[1]
    barrier, greeted = greet(at)
    load_in = pltpu.make_async_copy(w_in_hbm.at[0], w_in, weight_sem.at[0])
    load_out = pltpu.make_async_copy(w_out_hbm.at[0], w_out, weight_sem.at[1])
    load_in.start()
    load_out.start()

    own = (at["y"] // 2, at["z"], at["x"], at["y"] % 2, at["core"])
    chosen = chosen_ref[...]
    match_t = (
        lax.broadcasted_iota(jnp.int32, (experts_all, seq_len), 0) == chosen
    ).astype(jnp.float32)
    match = match_t.T
    match_low = match.astype(jnp.bfloat16)
    qkv_all[own] = qkv_ref[...]
    share = out_ref.shape[0]
    counts = jnp.dot(
        jnp.ones((share, seq_len), jnp.bfloat16), match_low, preferred_element_type=jnp.float32
    )
    out_all[own] = jnp.concatenate([out_ref[...], counts.astype(jnp.bfloat16)], axis=1)

    chunks, made_pieces = [], 0
    heads_wide = width // GROUPS
    beside = width + experts_all
    spans = [(qkv_all, g * heads_wide, heads_wide, width) for g in range(GROUPS)]
    spans.append((out_all, 0, beside // 3, beside // 3))
    for buf, first, wide, stride in spans:
        chunk = []
        for n, order in enumerate(ORDERS):
            cols = (first + n * stride, first + n * stride + wide)
            chunk.append(Piece(buf, cols, order, at, gather_send, gather_recv, 10 * made_pieces))
            made_pieces += 1
        chunks.append(chunk)

    pl.semaphore_wait(barrier, greeted)
    for chunk in chunks:
        for piece in chunk:
            piece.open(0)
    normed[...] = rms_scale(tokens_ref[...].astype(jnp.float32), gains_ref[0:1]).astype(
        jnp.bfloat16
    )
    for phase in (0, 1):
        for chunk in chunks:
            for piece in chunk:
                piece.arrive(phase)
                piece.open(phase + 1)

    row_ids = lax.broadcasted_iota(jnp.int32, (seq_len, seq_len), 0)
    col_ids = lax.broadcasted_iota(jnp.int32, (seq_len, seq_len), 1)
    lower = (col_ids < row_ids).astype(jnp.bfloat16)
    upper = (row_ids < col_ids).astype(jnp.bfloat16)
    rank_t = jnp.dot(match_t.astype(jnp.bfloat16), upper, preferred_element_type=jnp.float32)
    rank = jnp.dot(lower, match_low, preferred_element_type=jnp.float32)
    rank_col = jnp.sum(match * rank, axis=1, keepdims=True)
    slot_rows = sent.shape[1]
    first_t = shift_index(
        at, lax.broadcasted_iota(jnp.int32, (experts_all, seq_len), 0)
    ).astype(jnp.float32) * slot_rows
    first_row = shift_index(
        at, lax.broadcasted_iota(jnp.int32, (1, experts_all), 1)
    ).astype(jnp.float32) * slot_rows
    slot_row = jnp.sum(match_t * (rank_t + first_t), axis=0, keepdims=True).astype(jnp.int32)
    slot_col = jnp.sum(match * (rank + first_row), axis=1, keepdims=True).astype(jnp.int32)

    def hand_over(chunk):
        for piece in chunk:
            piece.arrive(2)
            piece.hand_over()

    def head_step(head, carry):
        lane = lax.broadcasted_iota(jnp.int32, (1, heads_wide), 1)
        size = width // HEADS
        here = jnp.where((lane // size) == head, 1.0, 0.0).astype(jnp.bfloat16)
        value = values[...] * here
        for half in range(2):
            rows = slice(half * seq_len // 2, (half + 1) * seq_len // 2)
            scores = lax.dot_general(
                queries[rows, :] * here, keys[...], (((1,), (1,)), ((), ())),
                preferred_element_type=jnp.float32,
            )
            weights = jnp.exp(scores - jnp.max(scores, axis=1, keepdims=True))
            norm = 1.0 / jnp.sum(weights, axis=1, keepdims=True)
            part = jnp.dot(weights.astype(jnp.bfloat16), value, preferred_element_type=jnp.float32)
            summed[rows, :] += part * norm
        return carry

    hand_over(chunks[0])
    per_group = HEADS // GROUPS
    scale = (width // HEADS) ** -0.5
    for g in range(GROUPS):
        for piece in chunks[g]:
            piece.taken_over()
        for n, target in enumerate((queries, keys, values)):
            first = n * width + g * heads_wide
            weight = qkv_all[:, :, :, :, :, :, first : first + heads_wide].reshape(width, heads_wide)
            product = jnp.dot(normed[...], weight, preferred_element_type=jnp.float32)
            product = product.astype(jnp.bfloat16)
            target[...] = product * jnp.bfloat16(scale) if n == 0 else product
        summed[...] = jnp.zeros_like(summed)
        lax.fori_loop(0, per_group // 2, head_step, 0)
        hand_over(chunks[g + 1])
        lax.fori_loop(per_group // 2, per_group, head_step, 0)
        context[:, g * heads_wide : (g + 1) * heads_wide] = summed[...].astype(jnp.bfloat16)

    for piece in chunks[GROUPS]:
        piece.taken_over()
    for g in range(GROUPS):
        span = slice(g * heads_wide, (g + 1) * heads_wide)
        weight = out_all[:, :, :, :, :, :, span].reshape(width, heads_wide)
        product = jnp.dot(context[...], weight, preferred_element_type=jnp.float32)
        hidden[:, span] = tokens_ref[:, span].astype(jnp.float32) + product
    normed[...] = rms_scale(hidden[...], gains_ref[1:2]).astype(jnp.bfloat16)

    blocks = sent.shape[0]
    per = blocks // STAGES
    rows = per * slot_rows

    def fill(stage):
        wanted = lax.broadcasted_iota(jnp.int32, (rows, seq_len), 0) + stage * rows
        pick = (wanted == slot_row).astype(jnp.bfloat16)
        block = jnp.dot(pick, normed[...], preferred_element_type=jnp.float32).astype(jnp.bfloat16)
        sent[pl.ds(stage * per, per)] = block.reshape(per, slot_rows, width)

    def send_stage(stage, source, target, way):
        def send_block(turn, step, dc):
            index = stage * per + turn * 8 + step * 2 + dc
            pltpu.make_async_remote_copy(
                src_ref=source.at[index],
                dst_ref=target.at[index],
                send_sem=send_sem.at[way],
                recv_sem=recv_sem.at[way, stage],
                device_id=device_of(shifted(at, stage, turn, step, dc, 1 - 2 * way)),
                device_id_type=MESH,
            ).start()

        def send_turn(turn, carry):
            for step in range(4):
                for dc in range(2):
                    if stage == 0 and step == 0 and dc == 0:
                        pl.when(turn > 0)(lambda: send_block(turn, 0, 0))
                    else:
                        send_block(turn, step, dc)
            return carry

        lax.fori_loop(0, 4, send_turn, 0)

    def stage_arrived(stage, target, way):
        first = 1 if stage == 0 else 0
        span = pl.ds(stage * per + first, per - first)
        pltpu.make_async_copy(target.at[span], target.at[span], recv_sem.at[way, stage]).wait()

    for stage in range(STAGES):
        fill(stage)
        if stage == 0:
            held[0] = sent[0]
        send_stage(stage, sent, held, 0)

    counts_all = out_all[:, :, :, :, :, :, width:beside].reshape(width, experts_all)
    row_of = lax.broadcasted_iota(jnp.int32, (8, width), 1)
    lower_rows = ((row_of % share == 0) & (row_of < me * share)).astype(jnp.bfloat16)
    before = jnp.dot(lower_rows, counts_all, preferred_element_type=jnp.float32)[0:1]
    dev_of = lax.broadcasted_iota(jnp.int32, (1, experts_all), 1) % (experts_all // 2)
    flagged = jnp.zeros((1, experts_all), jnp.int32)
    for n in range(swap_ref.shape[0]):
        flagged = jnp.maximum(flagged, (dev_of == swap_ref[n]).astype(jnp.int32))
    capacity = capacity_ref[...]
    half = experts_all // 2
    traded = jnp.concatenate([capacity[:, half:], capacity[:, :half]], axis=1)
    room = jnp.where(flagged > 0, traded, capacity).astype(jnp.float32) - before
    kept = rank_col < jnp.sum(match * room, axis=1, keepdims=True)
    logits = jnp.dot(normed[...], router_ref[...], preferred_element_type=jnp.float32)
    gate = jax.nn.sigmoid(jnp.sum(match * logits, axis=1, keepdims=True))
    gate = jnp.where(kept, gate, 0.0)
    load_in.wait()
    load_out.wait()
    total[...] = jnp.zeros_like(total)

    tile = 256
    for stage in range(STAGES):
        stage_arrived(stage, held, 0)
        block = held[pl.ds(stage * per, per)].reshape(rows, width)
        for t in range(w_in.shape[1] // tile):
            span = slice(t * tile, (t + 1) * tile)
            product = jnp.dot(block, w_in[:, span], preferred_element_type=jnp.float32)
            activ[:, span] = jnp.maximum(product, 0.0).astype(jnp.bfloat16)
        for t in range(width // tile):
            span = slice(t * tile, (t + 1) * tile)
            product = jnp.dot(activ[...], w_out[:, span], preferred_element_type=jnp.float32)
            made[pl.ds(stage * per, per), :, span] = product.astype(jnp.bfloat16).reshape(
                per, slot_rows, tile
            )
        send_stage(stage, made, back, 1)
    for stage in range(STAGES):
        stage_arrived(stage, back, 1)
        if stage == 0:
            back[0] = made[0]
        wanted = lax.broadcasted_iota(jnp.int32, (seq_len, rows), 1) + stage * rows
        pick = (wanted == slot_col).astype(jnp.bfloat16)
        block = back[pl.ds(stage * per, per)].reshape(rows, width)
        total[...] += jnp.dot(pick, block, preferred_element_type=jnp.float32)
    mixed_ref[...] = (hidden[...] + gate * total[...]).astype(jnp.bfloat16)
    for way, source in ((0, sent), (1, made)):
        span = pl.ds(1, blocks - 1)
        pltpu.make_async_copy(source.at[span], source.at[span], send_sem.at[way]).wait()
    for chunk in chunks:
        for piece in chunk:
            piece.drain()


def shards(
    tokens,
    expert_ids,
    w_qkv,
    w_attn_out,
    gain_attn,
    gain_expert,
    router,
    expert_in,
    expert_out,
    capacity,
    swap_list,
):
    seq_len, width = tokens.shape
    experts_all = router.shape[1]
    slot_rows = 2 * seq_len // experts_all
    lead = (2, 4, 4, 2, 2)
    low, wide = jnp.bfloat16, width // GROUPS
    exchange = pltpu.VMEM((experts_all, slot_rows, width), low)
    vmem = pl.BlockSpec(memory_space=pltpu.VMEM)
    hbm = pl.BlockSpec(memory_space=pl.ANY)
    copies = 10 * 3 * (GROUPS + 1)
    return pl.pallas_call(
        layer_kernel,
        out_shape=jax.ShapeDtypeStruct((seq_len, width), low),
        in_specs=[pl.BlockSpec(memory_space=pltpu.SMEM)] + [vmem] * 7 + [hbm] * 2,
        out_specs=vmem,
        scratch_shapes=[
            pltpu.VMEM(lead + w_qkv.shape, low),
            pltpu.VMEM(lead + (w_attn_out.shape[0], width + experts_all), low),
            pltpu.VMEM((seq_len, width), low),
            pltpu.VMEM((seq_len, wide), low),
            pltpu.VMEM((seq_len, wide), low),
            pltpu.VMEM((seq_len, wide), low),
            pltpu.VMEM((seq_len, wide), jnp.float32),
            pltpu.VMEM((seq_len, width), low),
            pltpu.VMEM((seq_len, width), jnp.float32),
            exchange,
            exchange,
            exchange,
            exchange,
            pltpu.VMEM(expert_in.shape[1:], low),
            pltpu.VMEM(expert_out.shape[1:], low),
            pltpu.VMEM((experts_all // STAGES * slot_rows, expert_in.shape[2]), low),
            pltpu.VMEM((seq_len, width), jnp.float32),
            pltpu.SemaphoreType.DMA((2,)),
            pltpu.SemaphoreType.DMA((copies,)),
            pltpu.SemaphoreType.DMA((copies,)),
            pltpu.SemaphoreType.DMA((2,)),
            pltpu.SemaphoreType.DMA((2, STAGES)),
        ],
        compiler_params=pltpu.CompilerParams(
            collective_id=0, has_side_effects=True, vmem_limit_bytes=58 << 20
        ),
        name="encoder_layer",
    )(
        swap_list, tokens, expert_ids.reshape(1, seq_len), w_qkv, w_attn_out,
        jnp.stack([gain_attn, gain_expert]).astype(jnp.float32), router, capacity[None, :], expert_in, expert_out,
    )


def solution(mesh):
    return jax.shard_map(
        shards,
        mesh=mesh,
        in_specs=(
            P(("role", "dev"), None),
            P(("role", "dev"), None),
            P(("role", "dev"), None),
            P(("role", "dev"), None),
            P(),
            P(),
            P(),
            P(("role", "dev"), None, None),
            P(("role", "dev"), None, None),
            P(),
            P(),
        ),
        out_specs=P(("role", "dev"), None),
        check_vma=False,
    )
```

```python
import jax
import jax.numpy as jnp
from jax import lax
from jax.experimental import pallas as pl
from jax.experimental.pallas import tpu as pltpu
from jax.sharding import PartitionSpec as P

HEADS = 16
MESH = pl.DeviceIdType.MESH
GROUPS = 4
STAGES = 4
ORDERS = (("z", "x", "y"), ("x", "y", "z"), ("y", "z", "x"))


def coordinates():
    role, dev = lax.axis_index("role"), lax.axis_index("dev")
    return {"z": dev // 16, "x": dev // 4 % 4, "y": role * 2 + dev // 2 % 2, "core": dev % 2}


def device_of(at):
    y = at["y"]
    return (y // 2, ((at["z"] * 4 + at["x"]) * 2 + y % 2) * 2 + at["core"])


def moved(at, axis, by):
    size = 2 if axis == "core" else 4
    return {**at, axis: (at[axis] + by) % size}


def block_of(buf, at, whole, cols):
    every = slice(None)
    yh, yl = (every, every) if "y" in whole else (at["y"] // 2, at["y"] % 2)
    z = every if "z" in whole else at["z"]
    x = every if "x" in whole else at["x"]
    return buf.at[yh, z, x, yl, at["core"], every, slice(*cols)]


TWICE = (0, 2, 3, 1)
THRICE = (0, 3, 1, 2)


def crossed(two_bits, mask):
    return (two_bits, two_bits + 1 - 2 * (two_bits % 2), (two_bits + 2) % 4, 3 - two_bits)[mask]


def shifted(at, stage, turn, step, dc, sign):
    dx = crossed(turn, TWICE[step])
    dy = crossed(stage, THRICE[step])
    return {
        "z": (at["z"] + 4 + sign * step) % 4,
        "x": (at["x"] + 4 + sign * dx) % 4,
        "y": (at["y"] + 4 + sign * dy) % 4,
        "core": (at["core"] + dc) % 2,
    }


def shift_index(at, expert):
    dz = ((expert >> 4) - at["z"] + 4) & 3
    dx = ((expert >> 2) - at["x"] + 4) & 3
    dy = ((expert >> 6) * 2 + ((expert >> 1) & 1) - at["y"] + 4) & 3
    dc = (expert - at["core"] + 2) & 1
    twice = ((dz >> 1) ^ (dz & 1)) * 2 + (dz >> 1)
    turn, stage = dx ^ twice, dy ^ twice ^ dz
    return stage * 32 + turn * 8 + dz * 2 + dc


class Piece:
    def __init__(self, buf, cols, order, at, send, recv, first):
        self.buf, self.cols, self.order, self.at = buf, cols, order, at
        self.send, self.recv, self.first = send, recv, first
        self.started = []

    def copy(self, block_at, whole, to, slot):
        ref = block_of(self.buf, block_at, whole, self.cols)
        return pltpu.make_async_remote_copy(
            src_ref=ref,
            dst_ref=ref,
            send_sem=self.send.at[self.first + slot],
            recv_sem=self.recv.at[self.first + slot],
            device_id=device_of(to),
            device_id_type=MESH,
        )

    def start(self, *args):
        copy = self.copy(*args)
        copy.start()
        self.started.append(copy)

    def open(self, phase):
        axis, whole = self.order[phase], self.order[:phase]
        for by in (1, 3, 2):
            self.start(self.at, whole, moved(self.at, axis, by), phase * 3 + by - 1)

    def arrive(self, phase):
        axis, whole = self.order[phase], self.order[:phase]
        for by in (1, 3, 2):
            source = moved(self.at, axis, -by % 4)
            self.copy(source, whole, source, phase * 3 + by - 1).wait_recv()

    def hand_over(self):
        self.start(self.at, self.order, moved(self.at, "core", 1), 9)

    def taken_over(self):
        other = moved(self.at, "core", 1)
        self.copy(other, self.order, other, 9).wait_recv()

    def drain(self):
        for copy in self.started:
            copy.wait_send()


def greet(at):
    barrier = pltpu.get_barrier_semaphore()
    near = [(axis, by) for axis in ("z", "x", "y") for by in (1, 2, 3)] + [("core", 1)]
    for axis, by in near:
        pl.semaphore_signal(
            barrier, inc=1, device_id=device_of(moved(at, axis, by)), device_id_type=MESH
        )
    return barrier, len(near)


def rms_scale(values, gain):
    mean_sq = jnp.mean(values * values, axis=-1, keepdims=True)
    return values * lax.rsqrt(mean_sq + 1e-06) * gain.astype(jnp.float32).reshape(1, -1)


def layer_kernel(
    swap_ref, tokens_hbm, chosen_ref, qkv_ref, out_ref, gain_attn_ref, gain_expert_ref, router_hbm,
    capacity_ref, w_in_hbm, w_out_hbm, mixed_ref,
    tokens_ref, router_ref, qkv_all, out_all, normed, queries, keys, values, summed, context, hidden,
    sent, held, made, back, w_in, w_out, activ, total,
    weight_sem, gather_send, gather_recv, send_sem, recv_sem,
):
    at = coordinates()
    me = lax.axis_index("role") * 64 + lax.axis_index("dev")
    seq_len, width = tokens_ref.shape
    experts_all = router_ref.shape[1]
    barrier, greeted = greet(at)
    load_in = pltpu.make_async_copy(w_in_hbm.at[0], w_in, weight_sem.at[0])
    load_out = pltpu.make_async_copy(w_out_hbm.at[0], w_out, weight_sem.at[1])
    load_tokens = pltpu.make_async_copy(tokens_hbm, tokens_ref, weight_sem.at[2])
    load_router = pltpu.make_async_copy(router_hbm, router_ref, weight_sem.at[3])
    load_tokens.start()
    load_router.start()
    load_in.start()
    load_out.start()

    own = (at["y"] // 2, at["z"], at["x"], at["y"] % 2, at["core"])
    chosen = chosen_ref[...]
    match_t = (
        lax.broadcasted_iota(jnp.int32, (experts_all, seq_len), 0) == chosen
    ).astype(jnp.float32)
    match = match_t.T
    match_low = match.astype(jnp.bfloat16)
    qkv_all[own] = qkv_ref[...]
    share = out_ref.shape[0]
    counts = jnp.dot(
        jnp.ones((share, seq_len), jnp.bfloat16), match_low, preferred_element_type=jnp.float32
    )
    out_all[own] = jnp.concatenate([out_ref[...], counts.astype(jnp.bfloat16)], axis=1)

    chunks, made_pieces = [], 0
    heads_wide = width // GROUPS
    beside = width + experts_all
    spans = [(qkv_all, g * heads_wide, heads_wide, width) for g in range(GROUPS)]
    spans.append((out_all, 0, beside // 3, beside // 3))
    for buf, first, wide, stride in spans:
        chunk = []
        for n, order in enumerate(ORDERS):
            cols = (first + n * stride, first + n * stride + wide)
            chunk.append(Piece(buf, cols, order, at, gather_send, gather_recv, 10 * made_pieces))
            made_pieces += 1
        chunks.append(chunk)

    pl.semaphore_wait(barrier, greeted)
    for chunk in chunks:
        for piece in chunk:
            piece.open(0)
    load_tokens.wait()
    normed[...] = rms_scale(tokens_ref[...].astype(jnp.float32), gain_attn_ref[...]).astype(
        jnp.bfloat16
    )
    for phase in (0, 1):
        for chunk in chunks:
            for piece in chunk:
                piece.arrive(phase)
                piece.open(phase + 1)

    row_ids = lax.broadcasted_iota(jnp.int32, (seq_len, seq_len), 0)
    col_ids = lax.broadcasted_iota(jnp.int32, (seq_len, seq_len), 1)
    lower = (col_ids < row_ids).astype(jnp.bfloat16)
    upper = (row_ids < col_ids).astype(jnp.bfloat16)
    rank_t = jnp.dot(match_t.astype(jnp.bfloat16), upper, preferred_element_type=jnp.float32)
    rank = jnp.dot(lower, match_low, preferred_element_type=jnp.float32)
    rank_col = jnp.sum(match * rank, axis=1, keepdims=True)
    slot_rows = sent.shape[1]
    first_t = shift_index(
        at, lax.broadcasted_iota(jnp.int32, (experts_all, seq_len), 0)
    ).astype(jnp.float32) * slot_rows
    first_row = shift_index(
        at, lax.broadcasted_iota(jnp.int32, (1, experts_all), 1)
    ).astype(jnp.float32) * slot_rows
    slot_row = jnp.sum(match_t * (rank_t + first_t), axis=0, keepdims=True).astype(jnp.int32)
    slot_col = jnp.sum(match * (rank + first_row), axis=1, keepdims=True).astype(jnp.int32)

    def hand_over(chunk):
        for piece in chunk:
            piece.arrive(2)
            piece.hand_over()

    def head_step(head, carry):
        lane = lax.broadcasted_iota(jnp.int32, (1, heads_wide), 1)
        size = width // HEADS
        here = jnp.where((lane // size) == head, 1.0, 0.0).astype(jnp.bfloat16)
        value = values[...] * here
        for half in range(2):
            rows = slice(half * seq_len // 2, (half + 1) * seq_len // 2)
            scores = lax.dot_general(
                queries[rows, :] * here, keys[...], (((1,), (1,)), ((), ())),
                preferred_element_type=jnp.float32,
            )
            weights = jnp.exp(scores - jnp.max(scores, axis=1, keepdims=True))
            norm = 1.0 / jnp.sum(weights, axis=1, keepdims=True)
            part = jnp.dot(weights.astype(jnp.bfloat16), value, preferred_element_type=jnp.float32)
            summed[rows, :] += part * norm
        return carry

    hand_over(chunks[0])
    per_group = HEADS // GROUPS
    scale = (width // HEADS) ** -0.5
    for g in range(GROUPS):
        for piece in chunks[g]:
            piece.taken_over()
        for n, target in enumerate((queries, keys, values)):
            first = n * width + g * heads_wide
            weight = qkv_all[:, :, :, :, :, :, first : first + heads_wide].reshape(width, heads_wide)
            product = jnp.dot(normed[...], weight, preferred_element_type=jnp.float32)
            product = product.astype(jnp.bfloat16)
            target[...] = product * jnp.bfloat16(scale) if n == 0 else product
        summed[...] = jnp.zeros_like(summed)
        hand_over(chunks[g + 1])
        lax.fori_loop(0, per_group, head_step, 0)
        context[:, g * heads_wide : (g + 1) * heads_wide] = summed[...].astype(jnp.bfloat16)

    for piece in chunks[GROUPS]:
        piece.taken_over()
    for g in range(GROUPS):
        span = slice(g * heads_wide, (g + 1) * heads_wide)
        weight = out_all[:, :, :, :, :, :, span].reshape(width, heads_wide)
        product = jnp.dot(context[...], weight, preferred_element_type=jnp.float32)
        hidden[:, span] = tokens_ref[:, span].astype(jnp.float32) + product
    normed[...] = rms_scale(hidden[...], gain_expert_ref[...]).astype(jnp.bfloat16)

    blocks = sent.shape[0]
    per = blocks // STAGES
    rows = per * slot_rows

    def fill(stage):
        wanted = lax.broadcasted_iota(jnp.int32, (rows, seq_len), 0) + stage * rows
        pick = (wanted == slot_row).astype(jnp.bfloat16)
        block = jnp.dot(pick, normed[...], preferred_element_type=jnp.float32).astype(jnp.bfloat16)
        sent[pl.ds(stage * per, per)] = block.reshape(per, slot_rows, width)

    def send_stage(stage, source, target, way):
        def send_block(turn, step, dc):
            index = stage * per + turn * 8 + step * 2 + dc
            pltpu.make_async_remote_copy(
                src_ref=source.at[index],
                dst_ref=target.at[index],
                send_sem=send_sem.at[way],
                recv_sem=recv_sem.at[way, stage],
                device_id=device_of(shifted(at, stage, turn, step, dc, 1 - 2 * way)),
                device_id_type=MESH,
            ).start()

        def send_turn(turn, carry):
            for step in range(4):
                for dc in range(2):
                    if stage == 0 and step == 0 and dc == 0:
                        pl.when(turn > 0)(lambda: send_block(turn, 0, 0))
                    else:
                        send_block(turn, step, dc)
            return carry

        lax.fori_loop(0, 4, send_turn, 0)

    def stage_arrived(stage, target, way):
        first = 1 if stage == 0 else 0
        span = pl.ds(stage * per + first, per - first)
        pltpu.make_async_copy(target.at[span], target.at[span], recv_sem.at[way, stage]).wait()

    for stage in range(STAGES):
        fill(stage)
        if stage == 0:
            held[0] = sent[0]
        send_stage(stage, sent, held, 0)

    counts_all = out_all[:, :, :, :, :, :, width:beside].reshape(width, experts_all)
    row_of = lax.broadcasted_iota(jnp.int32, (8, width), 1)
    lower_rows = ((row_of % share == 0) & (row_of < me * share)).astype(jnp.bfloat16)
    before = jnp.dot(lower_rows, counts_all, preferred_element_type=jnp.float32)[0:1]
    dev_of = lax.broadcasted_iota(jnp.int32, (1, experts_all), 1) % (experts_all // 2)
    flagged = jnp.zeros((1, experts_all), jnp.int32)
    for n in range(swap_ref.shape[0]):
        flagged = jnp.maximum(flagged, (dev_of == swap_ref[n]).astype(jnp.int32))
    capacity = capacity_ref[...]
    half = experts_all // 2
    traded = jnp.concatenate([capacity[:, half:], capacity[:, :half]], axis=1)
    room = jnp.where(flagged > 0, traded, capacity).astype(jnp.float32) - before
    kept = rank_col < jnp.sum(match * room, axis=1, keepdims=True)
    load_router.wait()
    logits = jnp.dot(normed[...], router_ref[...], preferred_element_type=jnp.float32)
    gate = jax.nn.sigmoid(jnp.sum(match * logits, axis=1, keepdims=True))
    gate = jnp.where(kept, gate, 0.0)
    load_in.wait()
    load_out.wait()
    total[...] = jnp.zeros_like(total)

    tile = 256
    for stage in range(STAGES):
        stage_arrived(stage, held, 0)
        block = held[pl.ds(stage * per, per)].reshape(rows, width)
        for t in range(w_in.shape[1] // tile):
            span = slice(t * tile, (t + 1) * tile)
            product = jnp.dot(block, w_in[:, span], preferred_element_type=jnp.float32)
            activ[:, span] = jnp.maximum(product, 0.0).astype(jnp.bfloat16)
        for t in range(width // tile):
            span = slice(t * tile, (t + 1) * tile)
            product = jnp.dot(activ[...], w_out[:, span], preferred_element_type=jnp.float32)
            made[pl.ds(stage * per, per), :, span] = product.astype(jnp.bfloat16).reshape(
                per, slot_rows, tile
            )
        send_stage(stage, made, back, 1)
    for stage in range(STAGES):
        stage_arrived(stage, back, 1)
        if stage == 0:
            back[0] = made[0]
        wanted = lax.broadcasted_iota(jnp.int32, (seq_len, rows), 1) + stage * rows
        pick = (wanted == slot_col).astype(jnp.bfloat16)
        block = back[pl.ds(stage * per, per)].reshape(rows, width)
        total[...] += jnp.dot(pick, block, preferred_element_type=jnp.float32)
    mixed_ref[...] = (hidden[...] + gate * total[...]).astype(jnp.bfloat16)
    for way, source in ((0, sent), (1, made)):
        span = pl.ds(1, blocks - 1)
        pltpu.make_async_copy(source.at[span], source.at[span], send_sem.at[way]).wait()
    for chunk in chunks:
        for piece in chunk:
            piece.drain()


def shards(
    tokens,
    expert_ids,
    w_qkv,
    w_attn_out,
    gain_attn,
    gain_expert,
    router,
    expert_in,
    expert_out,
    capacity,
    swap_list,
):
    seq_len, width = tokens.shape
    experts_all = router.shape[1]
    slot_rows = 2 * seq_len // experts_all
    lead = (2, 4, 4, 2, 2)
    low, wide = jnp.bfloat16, width // GROUPS
    exchange = pltpu.VMEM((experts_all, slot_rows, width), low)
    vmem = pl.BlockSpec(memory_space=pltpu.VMEM)
    hbm = pl.BlockSpec(memory_space=pl.ANY)
    copies = 10 * 3 * (GROUPS + 1)
    return pl.pallas_call(
        layer_kernel,
        out_shape=jax.ShapeDtypeStruct((seq_len, width), low),
        in_specs=[pl.BlockSpec(memory_space=pltpu.SMEM), hbm] + [vmem] * 5 + [hbm, vmem] + [hbm] * 2,
        out_specs=vmem,
        scratch_shapes=[
            pltpu.VMEM(tokens.shape, low),
            pltpu.VMEM(router.shape, low),
            pltpu.VMEM(lead + w_qkv.shape, low),
            pltpu.VMEM(lead + (w_attn_out.shape[0], width + experts_all), low),
            pltpu.VMEM((seq_len, width), low),
            pltpu.VMEM((seq_len, wide), low),
            pltpu.VMEM((seq_len, wide), low),
            pltpu.VMEM((seq_len, wide), low),
            pltpu.VMEM((seq_len, wide), jnp.float32),
            pltpu.VMEM((seq_len, width), low),
            pltpu.VMEM((seq_len, width), jnp.float32),
            exchange,
            exchange,
            exchange,
            exchange,
            pltpu.VMEM(expert_in.shape[1:], low),
            pltpu.VMEM(expert_out.shape[1:], low),
            pltpu.VMEM((experts_all // STAGES * slot_rows, expert_in.shape[2]), low),
            pltpu.VMEM((seq_len, width), jnp.float32),
            pltpu.SemaphoreType.DMA((4,)),
            pltpu.SemaphoreType.DMA((copies,)),
            pltpu.SemaphoreType.DMA((copies,)),
            pltpu.SemaphoreType.DMA((2,)),
            pltpu.SemaphoreType.DMA((2, STAGES)),
        ],
        compiler_params=pltpu.CompilerParams(
            collective_id=0, has_side_effects=True, vmem_limit_bytes=58 << 20
        ),
        name="encoder_layer",
    )(
        swap_list, tokens, expert_ids.reshape(1, seq_len), w_qkv, w_attn_out,
        gain_attn, gain_expert, router, capacity[None, :], expert_in, expert_out,
    )


def solution(mesh):
    return jax.shard_map(
        shards,
        mesh=mesh,
        in_specs=(
            P(("role", "dev"), None),
            P(("role", "dev"), None),
            P(("role", "dev"), None),
            P(("role", "dev"), None),
            P(),
            P(),
            P(),
            P(("role", "dev"), None, None),
            P(("role", "dev"), None, None),
            P(),
            P(),
        ),
        out_specs=P(("role", "dev"), None),
        check_vma=False,
    )
```

```python
import jax
import jax.numpy as jnp
from jax import lax
from jax.experimental import pallas as pl
from jax.experimental.pallas import tpu as pltpu
from jax.sharding import PartitionSpec as P

HEADS = 16
MESH = pl.DeviceIdType.MESH
GROUPS = 4
STAGES = 4
ORDERS = (("z", "x", "y"), ("x", "y", "z"), ("y", "z", "x"))


def coordinates():
    role, dev = lax.axis_index("role"), lax.axis_index("dev")
    return {"z": dev // 16, "x": dev // 4 % 4, "y": role * 2 + dev // 2 % 2, "core": dev % 2}


def device_of(at):
    y = at["y"]
    return (y // 2, ((at["z"] * 4 + at["x"]) * 2 + y % 2) * 2 + at["core"])


def moved(at, axis, by):
    size = 2 if axis == "core" else 4
    return {**at, axis: (at[axis] + by) % size}


def block_of(buf, at, whole, cols):
    every = slice(None)
    yh, yl = (every, every) if "y" in whole else (at["y"] // 2, at["y"] % 2)
    z = every if "z" in whole else at["z"]
    x = every if "x" in whole else at["x"]
    return buf.at[yh, z, x, yl, at["core"], every, slice(*cols)]


TWICE = (0, 2, 3, 1)
THRICE = (0, 3, 1, 2)


def crossed(two_bits, mask):
    return (two_bits, two_bits + 1 - 2 * (two_bits % 2), (two_bits + 2) % 4, 3 - two_bits)[mask]


def shifted(at, stage, turn, step, dc, sign):
    dx = crossed(turn, TWICE[step])
    dy = crossed(stage, THRICE[step])
    return {
        "z": (at["z"] + 4 + sign * step) % 4,
        "x": (at["x"] + 4 + sign * dx) % 4,
        "y": (at["y"] + 4 + sign * dy) % 4,
        "core": (at["core"] + dc) % 2,
    }


def shift_index(at, expert):
    dz = ((expert >> 4) - at["z"] + 4) & 3
    dx = ((expert >> 2) - at["x"] + 4) & 3
    dy = ((expert >> 6) * 2 + ((expert >> 1) & 1) - at["y"] + 4) & 3
    dc = (expert - at["core"] + 2) & 1
    twice = ((dz >> 1) ^ (dz & 1)) * 2 + (dz >> 1)
    turn, stage = dx ^ twice, dy ^ twice ^ dz
    return stage * 32 + turn * 8 + dz * 2 + dc


class Piece:
    def __init__(self, buf, cols, order, at, send, recv, first):
        self.buf, self.cols, self.order, self.at = buf, cols, order, at
        self.send, self.recv, self.first = send, recv, first
        self.started = []

    def copy(self, block_at, whole, to, slot):
        ref = block_of(self.buf, block_at, whole, self.cols)
        return pltpu.make_async_remote_copy(
            src_ref=ref,
            dst_ref=ref,
            send_sem=self.send.at[self.first + slot],
            recv_sem=self.recv.at[self.first + slot],
            device_id=device_of(to),
            device_id_type=MESH,
        )

    def start(self, *args):
        copy = self.copy(*args)
        copy.start()
        self.started.append(copy)

    def open(self, phase):
        axis, whole = self.order[phase], self.order[:phase]
        for by in (1, 3, 2):
            self.start(self.at, whole, moved(self.at, axis, by), phase * 3 + by - 1)

    def arrive(self, phase):
        axis, whole = self.order[phase], self.order[:phase]
        for by in (1, 3, 2):
            source = moved(self.at, axis, -by % 4)
            self.copy(source, whole, source, phase * 3 + by - 1).wait_recv()

    def hand_over(self):
        self.start(self.at, self.order, moved(self.at, "core", 1), 9)

    def taken_over(self):
        other = moved(self.at, "core", 1)
        self.copy(other, self.order, other, 9).wait_recv()

    def drain(self):
        for copy in self.started:
            copy.wait_send()


def greet(at):
    barrier = pltpu.get_barrier_semaphore()
    near = [(axis, by) for axis in ("z", "x", "y") for by in (1, 2, 3)] + [("core", 1)]
    for axis, by in near:
        pl.semaphore_signal(
            barrier, inc=1, device_id=device_of(moved(at, axis, by)), device_id_type=MESH
        )
    return barrier, len(near)


def rms_scale(values, gain):
    mean_sq = jnp.mean(values * values, axis=-1, keepdims=True)
    return values * lax.rsqrt(mean_sq + 1e-06) * gain.astype(jnp.float32).reshape(1, -1)


def layer_kernel(
    swap_ref, tokens_hbm, chosen_ref, qkv_ref, out_ref, gain_attn_ref, gain_expert_ref, router_hbm,
    capacity_ref, w_in_hbm, w_out_hbm, mixed_ref,
    tokens_ref, router_ref, qkv_all, out_all, normed, queries, keys, values, summed, context, hidden,
    sent, held, made, back, w_in, w_out, activ, total,
    weight_sem, gather_send, gather_recv, send_sem, recv_sem,
):
    at = coordinates()
    me = lax.axis_index("role") * 64 + lax.axis_index("dev")
    seq_len, width = tokens_ref.shape
    experts_all = router_ref.shape[1]
    barrier, greeted = greet(at)
    load_in = pltpu.make_async_copy(w_in_hbm.at[0], w_in, weight_sem.at[0])
    load_out = pltpu.make_async_copy(w_out_hbm.at[0], w_out, weight_sem.at[1])
    load_tokens = pltpu.make_async_copy(tokens_hbm, tokens_ref, weight_sem.at[2])
    load_router = pltpu.make_async_copy(router_hbm, router_ref, weight_sem.at[3])
    load_tokens.start()
    load_router.start()
    load_in.start()
    load_out.start()

    own = (at["y"] // 2, at["z"], at["x"], at["y"] % 2, at["core"])
    chosen = chosen_ref[...]
    match_t = (
        lax.broadcasted_iota(jnp.int32, (experts_all, seq_len), 0) == chosen
    ).astype(jnp.float32)
    match = match_t.T
    match_low = match.astype(jnp.bfloat16)
    qkv_all[own] = qkv_ref[...]
    share = out_ref.shape[0]
    counts = jnp.dot(
        jnp.ones((share, seq_len), jnp.bfloat16), match_low, preferred_element_type=jnp.float32
    )
    out_all[own] = jnp.concatenate([out_ref[...], counts.astype(jnp.bfloat16)], axis=1)

    chunks, made_pieces = [], 0
    heads_wide = width // GROUPS
    beside = width + experts_all
    spans = [(qkv_all, g * heads_wide, heads_wide, width) for g in range(GROUPS)]
    spans.append((out_all, 0, beside // 3, beside // 3))
    for buf, first, wide, stride in spans:
        chunk = []
        for n, order in enumerate(ORDERS):
            cols = (first + n * stride, first + n * stride + wide)
            chunk.append(Piece(buf, cols, order, at, gather_send, gather_recv, 10 * made_pieces))
            made_pieces += 1
        chunks.append(chunk)

    pl.semaphore_wait(barrier, greeted)
    for chunk in chunks:
        for piece in chunk:
            piece.open(0)
    load_tokens.wait()
    normed[...] = rms_scale(tokens_ref[...].astype(jnp.float32), gain_attn_ref[...]).astype(
        jnp.bfloat16
    )
    for turn in range(len(chunks) + 1):
        for phase, number in ((0, turn), (1, turn - 1)):
            if 0 <= number < len(chunks):
                for piece in chunks[number]:
                    piece.arrive(phase)
                    piece.open(phase + 1)

    row_ids = lax.broadcasted_iota(jnp.int32, (seq_len, seq_len), 0)
    col_ids = lax.broadcasted_iota(jnp.int32, (seq_len, seq_len), 1)
    lower = (col_ids < row_ids).astype(jnp.bfloat16)
    upper = (row_ids < col_ids).astype(jnp.bfloat16)
    rank_t = jnp.dot(match_t.astype(jnp.bfloat16), upper, preferred_element_type=jnp.float32)
    rank = jnp.dot(lower, match_low, preferred_element_type=jnp.float32)
    rank_col = jnp.sum(match * rank, axis=1, keepdims=True)
    slot_rows = sent.shape[1]
    first_t = shift_index(
        at, lax.broadcasted_iota(jnp.int32, (experts_all, seq_len), 0)
    ).astype(jnp.float32) * slot_rows
    first_row = shift_index(
        at, lax.broadcasted_iota(jnp.int32, (1, experts_all), 1)
    ).astype(jnp.float32) * slot_rows
    slot_row = jnp.sum(match_t * (rank_t + first_t), axis=0, keepdims=True).astype(jnp.int32)
    slot_col = jnp.sum(match * (rank + first_row), axis=1, keepdims=True).astype(jnp.int32)

    def hand_over(chunk):
        for piece in chunk:
            piece.arrive(2)
            piece.hand_over()

    def head_step(head, carry):
        lane = lax.broadcasted_iota(jnp.int32, (1, heads_wide), 1)
        size = width // HEADS
        here = jnp.where((lane // size) == head, 1.0, 0.0).astype(jnp.bfloat16)
        value = values[...] * here
        for half in range(2):
            rows = slice(half * seq_len // 2, (half + 1) * seq_len // 2)
            scores = lax.dot_general(
                queries[rows, :] * here, keys[...], (((1,), (1,)), ((), ())),
                preferred_element_type=jnp.float32,
            )
            weights = jnp.exp(scores - jnp.max(scores, axis=1, keepdims=True))
            norm = 1.0 / jnp.sum(weights, axis=1, keepdims=True)
            part = jnp.dot(weights.astype(jnp.bfloat16), value, preferred_element_type=jnp.float32)
            summed[rows, :] += part * norm
        return carry

    hand_over(chunks[0])
    per_group = HEADS // GROUPS
    scale = (width // HEADS) ** -0.5
    for g in range(GROUPS):
        for piece in chunks[g]:
            piece.taken_over()
        for n, target in enumerate((queries, keys, values)):
            first = n * width + g * heads_wide
            weight = qkv_all[:, :, :, :, :, :, first : first + heads_wide].reshape(width, heads_wide)
            product = jnp.dot(normed[...], weight, preferred_element_type=jnp.float32)
            product = product.astype(jnp.bfloat16)
            target[...] = product * jnp.bfloat16(scale) if n == 0 else product
        summed[...] = jnp.zeros_like(summed)
        hand_over(chunks[g + 1])
        lax.fori_loop(0, per_group, head_step, 0)
        context[:, g * heads_wide : (g + 1) * heads_wide] = summed[...].astype(jnp.bfloat16)

    for piece in chunks[GROUPS]:
        piece.taken_over()
    for g in range(GROUPS):
        span = slice(g * heads_wide, (g + 1) * heads_wide)
        weight = out_all[:, :, :, :, :, :, span].reshape(width, heads_wide)
        product = jnp.dot(context[...], weight, preferred_element_type=jnp.float32)
        hidden[:, span] = tokens_ref[:, span].astype(jnp.float32) + product
    normed[...] = rms_scale(hidden[...], gain_expert_ref[...]).astype(jnp.bfloat16)

    blocks = sent.shape[0]
    per = blocks // STAGES
    rows = per * slot_rows

    def fill(stage):
        wanted = lax.broadcasted_iota(jnp.int32, (rows, seq_len), 0) + stage * rows
        pick = (wanted == slot_row).astype(jnp.bfloat16)
        block = jnp.dot(pick, normed[...], preferred_element_type=jnp.float32).astype(jnp.bfloat16)
        sent[pl.ds(stage * per, per)] = block.reshape(per, slot_rows, width)

    def send_stage(stage, source, target, way):
        def send_block(turn, step, dc):
            index = stage * per + turn * 8 + step * 2 + dc
            pltpu.make_async_remote_copy(
                src_ref=source.at[index],
                dst_ref=target.at[index],
                send_sem=send_sem.at[way],
                recv_sem=recv_sem.at[way, stage],
                device_id=device_of(shifted(at, stage, turn, step, dc, 1 - 2 * way)),
                device_id_type=MESH,
            ).start()

        def send_turn(turn, carry):
            for step in range(4):
                for dc in range(2):
                    if stage == 0 and step == 0 and dc == 0:
                        pl.when(turn > 0)(lambda: send_block(turn, 0, 0))
                    else:
                        send_block(turn, step, dc)
            return carry

        lax.fori_loop(0, 4, send_turn, 0)

    def stage_arrived(stage, target, way):
        first = 1 if stage == 0 else 0
        span = pl.ds(stage * per + first, per - first)
        pltpu.make_async_copy(target.at[span], target.at[span], recv_sem.at[way, stage]).wait()

    for stage in range(STAGES):
        fill(stage)
        if stage == 0:
            held[0] = sent[0]
        send_stage(stage, sent, held, 0)

    counts_all = out_all[:, :, :, :, :, :, width:beside].reshape(width, experts_all)
    row_of = lax.broadcasted_iota(jnp.int32, (8, width), 1)
    lower_rows = ((row_of % share == 0) & (row_of < me * share)).astype(jnp.bfloat16)
    before = jnp.dot(lower_rows, counts_all, preferred_element_type=jnp.float32)[0:1]
    dev_of = lax.broadcasted_iota(jnp.int32, (1, experts_all), 1) % (experts_all // 2)
    flagged = jnp.zeros((1, experts_all), jnp.int32)
    for n in range(swap_ref.shape[0]):
        flagged = jnp.maximum(flagged, (dev_of == swap_ref[n]).astype(jnp.int32))
    capacity = capacity_ref[...]
    half = experts_all // 2
    traded = jnp.concatenate([capacity[:, half:], capacity[:, :half]], axis=1)
    room = jnp.where(flagged > 0, traded, capacity).astype(jnp.float32) - before
    kept = rank_col < jnp.sum(match * room, axis=1, keepdims=True)
    load_router.wait()
    logits = jnp.dot(normed[...], router_ref[...], preferred_element_type=jnp.float32)
    gate = jax.nn.sigmoid(jnp.sum(match * logits, axis=1, keepdims=True))
    gate = jnp.where(kept, gate, 0.0)
    load_in.wait()
    load_out.wait()
    total[...] = jnp.zeros_like(total)

    tile = 256
    for stage in range(STAGES):
        stage_arrived(stage, held, 0)
        block = held[pl.ds(stage * per, per)].reshape(rows, width)
        for t in range(w_in.shape[1] // tile):
            span = slice(t * tile, (t + 1) * tile)
            product = jnp.dot(block, w_in[:, span], preferred_element_type=jnp.float32)
            activ[:, span] = jnp.maximum(product, 0.0).astype(jnp.bfloat16)
        for t in range(width // tile):
            span = slice(t * tile, (t + 1) * tile)
            product = jnp.dot(activ[...], w_out[:, span], preferred_element_type=jnp.float32)
            made[pl.ds(stage * per, per), :, span] = product.astype(jnp.bfloat16).reshape(
                per, slot_rows, tile
            )
        send_stage(stage, made, back, 1)
    for stage in range(STAGES):
        stage_arrived(stage, back, 1)
        if stage == 0:
            back[0] = made[0]
        wanted = lax.broadcasted_iota(jnp.int32, (seq_len, rows), 1) + stage * rows
        pick = (wanted == slot_col).astype(jnp.bfloat16)
        block = back[pl.ds(stage * per, per)].reshape(rows, width)
        total[...] += jnp.dot(pick, block, preferred_element_type=jnp.float32)
    mixed_ref[...] = (hidden[...] + gate * total[...]).astype(jnp.bfloat16)
    for way, source in ((0, sent), (1, made)):
        span = pl.ds(1, blocks - 1)
        pltpu.make_async_copy(source.at[span], source.at[span], send_sem.at[way]).wait()
    for chunk in chunks:
        for piece in chunk:
            piece.drain()


def shards(
    tokens,
    expert_ids,
    w_qkv,
    w_attn_out,
    gain_attn,
    gain_expert,
    router,
    expert_in,
    expert_out,
    capacity,
    swap_list,
):
    seq_len, width = tokens.shape
    experts_all = router.shape[1]
    slot_rows = 2 * seq_len // experts_all
    lead = (2, 4, 4, 2, 2)
    low, wide = jnp.bfloat16, width // GROUPS
    exchange = pltpu.VMEM((experts_all, slot_rows, width), low)
    vmem = pl.BlockSpec(memory_space=pltpu.VMEM)
    hbm = pl.BlockSpec(memory_space=pl.ANY)
    copies = 10 * 3 * (GROUPS + 1)
    return pl.pallas_call(
        layer_kernel,
        out_shape=jax.ShapeDtypeStruct((seq_len, width), low),
        in_specs=[pl.BlockSpec(memory_space=pltpu.SMEM), hbm] + [vmem] * 5 + [hbm, vmem] + [hbm] * 2,
        out_specs=vmem,
        scratch_shapes=[
            pltpu.VMEM(tokens.shape, low),
            pltpu.VMEM(router.shape, low),
            pltpu.VMEM(lead + w_qkv.shape, low),
            pltpu.VMEM(lead + (w_attn_out.shape[0], width + experts_all), low),
            pltpu.VMEM((seq_len, width), low),
            pltpu.VMEM((seq_len, wide), low),
            pltpu.VMEM((seq_len, wide), low),
            pltpu.VMEM((seq_len, wide), low),
            pltpu.VMEM((seq_len, wide), jnp.float32),
            pltpu.VMEM((seq_len, width), low),
            pltpu.VMEM((seq_len, width), jnp.float32),
            exchange,
            exchange,
            exchange,
            exchange,
            pltpu.VMEM(expert_in.shape[1:], low),
            pltpu.VMEM(expert_out.shape[1:], low),
            pltpu.VMEM((experts_all // STAGES * slot_rows, expert_in.shape[2]), low),
            pltpu.VMEM((seq_len, width), jnp.float32),
            pltpu.SemaphoreType.DMA((4,)),
            pltpu.SemaphoreType.DMA((copies,)),
            pltpu.SemaphoreType.DMA((copies,)),
            pltpu.SemaphoreType.DMA((2,)),
            pltpu.SemaphoreType.DMA((2, STAGES)),
        ],
        compiler_params=pltpu.CompilerParams(
            collective_id=0, has_side_effects=True, vmem_limit_bytes=58 << 20
        ),
        name="encoder_layer",
    )(
        swap_list, tokens, expert_ids.reshape(1, seq_len), w_qkv, w_attn_out,
        gain_attn, gain_expert, router, capacity[None, :], expert_in, expert_out,
    )


def solution(mesh):
    return jax.shard_map(
        shards,
        mesh=mesh,
        in_specs=(
            P(("role", "dev"), None),
            P(("role", "dev"), None),
            P(("role", "dev"), None),
            P(("role", "dev"), None),
            P(),
            P(),
            P(),
            P(("role", "dev"), None, None),
            P(("role", "dev"), None, None),
            P(),
            P(),
        ),
        out_specs=P(("role", "dev"), None),
        check_vma=False,
    )
```

```python
import jax
import jax.numpy as jnp
from jax import lax
from jax.experimental import pallas as pl
from jax.experimental.pallas import tpu as pltpu
from jax.sharding import PartitionSpec as P

HEADS = 16
MESH = pl.DeviceIdType.MESH
GROUPS = 4
STAGES = 4
ORDERS = (("z", "x", "y"), ("x", "y", "z"), ("y", "z", "x"))


def coordinates():
    role, dev = lax.axis_index("role"), lax.axis_index("dev")
    return {"z": dev // 16, "x": dev // 4 % 4, "y": role * 2 + dev // 2 % 2, "core": dev % 2}


def device_of(at):
    y = at["y"]
    return (y // 2, ((at["z"] * 4 + at["x"]) * 2 + y % 2) * 2 + at["core"])


def moved(at, axis, by):
    size = 2 if axis == "core" else 4
    return {**at, axis: (at[axis] + by) % size}


def block_of(buf, at, whole, cols):
    every = slice(None)
    yh, yl = (every, every) if "y" in whole else (at["y"] // 2, at["y"] % 2)
    z = every if "z" in whole else at["z"]
    x = every if "x" in whole else at["x"]
    return buf.at[yh, z, x, yl, at["core"], every, slice(*cols)]


TWICE = (0, 2, 3, 1)
THRICE = (0, 3, 1, 2)


def crossed(two_bits, mask):
    return (two_bits, two_bits + 1 - 2 * (two_bits % 2), (two_bits + 2) % 4, 3 - two_bits)[mask]


def shifted(at, stage, turn, step, dc, sign):
    dx = crossed(turn, TWICE[step])
    dy = crossed(stage, THRICE[step])
    return {
        "z": (at["z"] + 4 + sign * step) % 4,
        "x": (at["x"] + 4 + sign * dx) % 4,
        "y": (at["y"] + 4 + sign * dy) % 4,
        "core": (at["core"] + dc) % 2,
    }


def shift_index(at, expert):
    dz = ((expert >> 4) - at["z"] + 4) & 3
    dx = ((expert >> 2) - at["x"] + 4) & 3
    dy = ((expert >> 6) * 2 + ((expert >> 1) & 1) - at["y"] + 4) & 3
    dc = (expert - at["core"] + 2) & 1
    twice = ((dz >> 1) ^ (dz & 1)) * 2 + (dz >> 1)
    turn, stage = dx ^ twice, dy ^ twice ^ dz
    return stage * 32 + turn * 8 + dz * 2 + dc


class Piece:
    def __init__(self, buf, cols, order, at, send, recv, first):
        self.buf, self.cols, self.order, self.at = buf, cols, order, at
        self.send, self.recv, self.first = send, recv, first
        self.started = []

    def copy(self, block_at, whole, to, slot):
        ref = block_of(self.buf, block_at, whole, self.cols)
        return pltpu.make_async_remote_copy(
            src_ref=ref,
            dst_ref=ref,
            send_sem=self.send.at[self.first + slot],
            recv_sem=self.recv.at[self.first + slot],
            device_id=device_of(to),
            device_id_type=MESH,
        )

    def start(self, *args):
        copy = self.copy(*args)
        copy.start()
        self.started.append(copy)

    def open(self, phase):
        axis, whole = self.order[phase], self.order[:phase]
        for by in (1, 3, 2):
            self.start(self.at, whole, moved(self.at, axis, by), phase * 3 + by - 1)

    def arrive(self, phase):
        axis, whole = self.order[phase], self.order[:phase]
        for by in (1, 3, 2):
            source = moved(self.at, axis, -by % 4)
            self.copy(source, whole, source, phase * 3 + by - 1).wait_recv()

    def hand_over(self):
        self.start(self.at, self.order, moved(self.at, "core", 1), 9)

    def taken_over(self):
        other = moved(self.at, "core", 1)
        self.copy(other, self.order, other, 9).wait_recv()

    def drain(self):
        for copy in self.started:
            copy.wait_send()


def greet(at):
    barrier = pltpu.get_barrier_semaphore()
    near = [(axis, by) for axis in ("z", "x", "y") for by in (1, 2, 3)] + [("core", 1)]
    for axis, by in near:
        pl.semaphore_signal(
            barrier, inc=1, device_id=device_of(moved(at, axis, by)), device_id_type=MESH
        )
    return barrier, len(near)


def rms_scale(values, gain):
    mean_sq = jnp.mean(values * values, axis=-1, keepdims=True)
    return values * lax.rsqrt(mean_sq + 1e-06) * gain.astype(jnp.float32).reshape(1, -1)


def layer_kernel(
    swap_ref, tokens_hbm, chosen_ref, qkv_ref, out_ref, gain_attn_ref, gain_expert_ref, router_hbm,
    capacity_ref, w_in_hbm, w_out_hbm, mixed_ref,
    tokens_ref, router_ref, qkv_all, out_all, normed, queries, keys, values, summed, context, hidden,
    sent, held, made, back, w_in, w_out, activ, total,
    weight_sem, gather_send, gather_recv, send_sem, recv_sem,
):
    at = coordinates()
    me = lax.axis_index("role") * 64 + lax.axis_index("dev")
    seq_len, width = tokens_ref.shape
    experts_all = router_ref.shape[1]
    barrier, greeted = greet(at)
    load_in = pltpu.make_async_copy(w_in_hbm.at[0], w_in, weight_sem.at[0])
    load_out = pltpu.make_async_copy(w_out_hbm.at[0], w_out, weight_sem.at[1])
    load_tokens = pltpu.make_async_copy(tokens_hbm, tokens_ref, weight_sem.at[2])
    load_router = pltpu.make_async_copy(router_hbm, router_ref, weight_sem.at[3])
    load_tokens.start()
    load_router.start()
    load_in.start()
    load_out.start()

    own = (at["y"] // 2, at["z"], at["x"], at["y"] % 2, at["core"])
    chosen = chosen_ref[...]
    match_t = (
        lax.broadcasted_iota(jnp.int32, (experts_all, seq_len), 0) == chosen
    ).astype(jnp.float32)
    match = match_t.T
    match_low = match.astype(jnp.bfloat16)
    qkv_all[own] = qkv_ref[...]
    share = out_ref.shape[0]
    counts = jnp.dot(
        jnp.ones((share, seq_len), jnp.bfloat16), match_low, preferred_element_type=jnp.float32
    )
    out_all[own] = jnp.concatenate([out_ref[...], counts.astype(jnp.bfloat16)], axis=1)

    chunks, made_pieces = [], 0
    heads_wide = width // GROUPS
    beside = width + experts_all
    spans = [(qkv_all, g * heads_wide, heads_wide, width) for g in range(GROUPS)]
    spans.append((out_all, 0, beside // 3, beside // 3))
    for buf, first, wide, stride in spans:
        chunk = []
        for n, order in enumerate(ORDERS):
            cols = (first + n * stride, first + n * stride + wide)
            chunk.append(Piece(buf, cols, order, at, gather_send, gather_recv, 10 * made_pieces))
            made_pieces += 1
        chunks.append(chunk)

    pl.semaphore_wait(barrier, greeted)
    for chunk in chunks:
        for piece in chunk:
            piece.open(0)
    load_tokens.wait()
    normed[...] = rms_scale(tokens_ref[...].astype(jnp.float32), gain_attn_ref[...]).astype(
        jnp.bfloat16
    )
    for phase in (0, 1):
        for chunk in chunks:
            for piece in chunk:
                piece.arrive(phase)
                if phase == 0:
                    piece.open(1)
    for chunk in chunks[:2]:
        for piece in chunk:
            piece.open(2)

    row_ids = lax.broadcasted_iota(jnp.int32, (seq_len, seq_len), 0)
    col_ids = lax.broadcasted_iota(jnp.int32, (seq_len, seq_len), 1)
    lower = (col_ids < row_ids).astype(jnp.bfloat16)
    upper = (row_ids < col_ids).astype(jnp.bfloat16)
    rank_t = jnp.dot(match_t.astype(jnp.bfloat16), upper, preferred_element_type=jnp.float32)
    rank = jnp.dot(lower, match_low, preferred_element_type=jnp.float32)
    rank_col = jnp.sum(match * rank, axis=1, keepdims=True)
    slot_rows = sent.shape[1]
    first_t = shift_index(
        at, lax.broadcasted_iota(jnp.int32, (experts_all, seq_len), 0)
    ).astype(jnp.float32) * slot_rows
    first_row = shift_index(
        at, lax.broadcasted_iota(jnp.int32, (1, experts_all), 1)
    ).astype(jnp.float32) * slot_rows
    slot_row = jnp.sum(match_t * (rank_t + first_t), axis=0, keepdims=True).astype(jnp.int32)
    slot_col = jnp.sum(match * (rank + first_row), axis=1, keepdims=True).astype(jnp.int32)

    def hand_over(chunk):
        for piece in chunk:
            piece.arrive(2)
            piece.hand_over()

    def open_last(number):
        for piece in chunks[number] if number < len(chunks) else ():
            piece.open(2)

    def head_step(head, carry):
        lane = lax.broadcasted_iota(jnp.int32, (1, heads_wide), 1)
        size = width // HEADS
        here = jnp.where((lane // size) == head, 1.0, 0.0).astype(jnp.bfloat16)
        value = values[...] * here
        for half in range(2):
            rows = slice(half * seq_len // 2, (half + 1) * seq_len // 2)
            scores = lax.dot_general(
                queries[rows, :] * here, keys[...], (((1,), (1,)), ((), ())),
                preferred_element_type=jnp.float32,
            )
            weights = jnp.exp(scores - jnp.max(scores, axis=1, keepdims=True))
            norm = 1.0 / jnp.sum(weights, axis=1, keepdims=True)
            part = jnp.dot(weights.astype(jnp.bfloat16), value, preferred_element_type=jnp.float32)
            summed[rows, :] += part * norm
        return carry

    hand_over(chunks[0])
    open_last(2)
    per_group = HEADS // GROUPS
    scale = (width // HEADS) ** -0.5
    for g in range(GROUPS):
        for piece in chunks[g]:
            piece.taken_over()
        for n, target in enumerate((queries, keys, values)):
            first = n * width + g * heads_wide
            weight = qkv_all[:, :, :, :, :, :, first : first + heads_wide].reshape(width, heads_wide)
            product = jnp.dot(normed[...], weight, preferred_element_type=jnp.float32)
            product = product.astype(jnp.bfloat16)
            target[...] = product * jnp.bfloat16(scale) if n == 0 else product
        summed[...] = jnp.zeros_like(summed)
        hand_over(chunks[g + 1])
        open_last(g + 3)
        lax.fori_loop(0, per_group, head_step, 0)
        context[:, g * heads_wide : (g + 1) * heads_wide] = summed[...].astype(jnp.bfloat16)

    for piece in chunks[GROUPS]:
        piece.taken_over()
    for g in range(GROUPS):
        span = slice(g * heads_wide, (g + 1) * heads_wide)
        weight = out_all[:, :, :, :, :, :, span].reshape(width, heads_wide)
        product = jnp.dot(context[...], weight, preferred_element_type=jnp.float32)
        hidden[:, span] = tokens_ref[:, span].astype(jnp.float32) + product
    normed[...] = rms_scale(hidden[...], gain_expert_ref[...]).astype(jnp.bfloat16)

    blocks = sent.shape[0]
    per = blocks // STAGES
    rows = per * slot_rows

    def fill(stage):
        wanted = lax.broadcasted_iota(jnp.int32, (rows, seq_len), 0) + stage * rows
        pick = (wanted == slot_row).astype(jnp.bfloat16)
        block = jnp.dot(pick, normed[...], preferred_element_type=jnp.float32).astype(jnp.bfloat16)
        sent[pl.ds(stage * per, per)] = block.reshape(per, slot_rows, width)

    def send_stage(stage, source, target, way):
        def send_block(turn, step, dc):
            index = stage * per + turn * 8 + step * 2 + dc
            pltpu.make_async_remote_copy(
                src_ref=source.at[index],
                dst_ref=target.at[index],
                send_sem=send_sem.at[way],
                recv_sem=recv_sem.at[way, stage],
                device_id=device_of(shifted(at, stage, turn, step, dc, 1 - 2 * way)),
                device_id_type=MESH,
            ).start()

        def send_turn(turn, carry):
            for step in range(4):
                for dc in range(2):
                    if stage == 0 and step == 0 and dc == 0:
                        pl.when(turn > 0)(lambda: send_block(turn, 0, 0))
                    else:
                        send_block(turn, step, dc)
            return carry

        lax.fori_loop(0, 4, send_turn, 0)

    def stage_arrived(stage, target, way):
        first = 1 if stage == 0 else 0
        span = pl.ds(stage * per + first, per - first)
        pltpu.make_async_copy(target.at[span], target.at[span], recv_sem.at[way, stage]).wait()

    for stage in range(STAGES):
        fill(stage)
        if stage == 0:
            held[0] = sent[0]
        send_stage(stage, sent, held, 0)

    counts_all = out_all[:, :, :, :, :, :, width:beside].reshape(width, experts_all)
    row_of = lax.broadcasted_iota(jnp.int32, (8, width), 1)
    lower_rows = ((row_of % share == 0) & (row_of < me * share)).astype(jnp.bfloat16)
    before = jnp.dot(lower_rows, counts_all, preferred_element_type=jnp.float32)[0:1]
    dev_of = lax.broadcasted_iota(jnp.int32, (1, experts_all), 1) % (experts_all // 2)
    flagged = jnp.zeros((1, experts_all), jnp.int32)
    for n in range(swap_ref.shape[0]):
        flagged = jnp.maximum(flagged, (dev_of == swap_ref[n]).astype(jnp.int32))
    capacity = capacity_ref[...]
    half = experts_all // 2
    traded = jnp.concatenate([capacity[:, half:], capacity[:, :half]], axis=1)
    room = jnp.where(flagged > 0, traded, capacity).astype(jnp.float32) - before
    kept = rank_col < jnp.sum(match * room, axis=1, keepdims=True)
    load_router.wait()
    logits = jnp.dot(normed[...], router_ref[...], preferred_element_type=jnp.float32)
    gate = jax.nn.sigmoid(jnp.sum(match * logits, axis=1, keepdims=True))
    gate = jnp.where(kept, gate, 0.0)
    load_in.wait()
    load_out.wait()
    total[...] = jnp.zeros_like(total)

    tile = 256
    for stage in range(STAGES):
        stage_arrived(stage, held, 0)
        block = held[pl.ds(stage * per, per)].reshape(rows, width)
        for t in range(w_in.shape[1] // tile):
            span = slice(t * tile, (t + 1) * tile)
            product = jnp.dot(block, w_in[:, span], preferred_element_type=jnp.float32)
            activ[:, span] = jnp.maximum(product, 0.0).astype(jnp.bfloat16)
        for t in range(width // tile):
            span = slice(t * tile, (t + 1) * tile)
            product = jnp.dot(activ[...], w_out[:, span], preferred_element_type=jnp.float32)
            made[pl.ds(stage * per, per), :, span] = product.astype(jnp.bfloat16).reshape(
                per, slot_rows, tile
            )
        send_stage(stage, made, back, 1)
    for stage in range(STAGES):
        stage_arrived(stage, back, 1)
        if stage == 0:
            back[0] = made[0]
        wanted = lax.broadcasted_iota(jnp.int32, (seq_len, rows), 1) + stage * rows
        pick = (wanted == slot_col).astype(jnp.bfloat16)
        block = back[pl.ds(stage * per, per)].reshape(rows, width)
        total[...] += jnp.dot(pick, block, preferred_element_type=jnp.float32)
    mixed_ref[...] = (hidden[...] + gate * total[...]).astype(jnp.bfloat16)
    for way, source in ((0, sent), (1, made)):
        span = pl.ds(1, blocks - 1)
        pltpu.make_async_copy(source.at[span], source.at[span], send_sem.at[way]).wait()
    for chunk in chunks:
        for piece in chunk:
            piece.drain()


def shards(
    tokens,
    expert_ids,
    w_qkv,
    w_attn_out,
    gain_attn,
    gain_expert,
    router,
    expert_in,
    expert_out,
    capacity,
    swap_list,
):
    seq_len, width = tokens.shape
    experts_all = router.shape[1]
    slot_rows = 2 * seq_len // experts_all
    lead = (2, 4, 4, 2, 2)
    low, wide = jnp.bfloat16, width // GROUPS
    exchange = pltpu.VMEM((experts_all, slot_rows, width), low)
    vmem = pl.BlockSpec(memory_space=pltpu.VMEM)
    hbm = pl.BlockSpec(memory_space=pl.ANY)
    copies = 10 * 3 * (GROUPS + 1)
    return pl.pallas_call(
        layer_kernel,
        out_shape=jax.ShapeDtypeStruct((seq_len, width), low),
        in_specs=[pl.BlockSpec(memory_space=pltpu.SMEM), hbm] + [vmem] * 5 + [hbm, vmem] + [hbm] * 2,
        out_specs=vmem,
        scratch_shapes=[
            pltpu.VMEM(tokens.shape, low),
            pltpu.VMEM(router.shape, low),
            pltpu.VMEM(lead + w_qkv.shape, low),
            pltpu.VMEM(lead + (w_attn_out.shape[0], width + experts_all), low),
            pltpu.VMEM((seq_len, width), low),
            pltpu.VMEM((seq_len, wide), low),
            pltpu.VMEM((seq_len, wide), low),
            pltpu.VMEM((seq_len, wide), low),
            pltpu.VMEM((seq_len, wide), jnp.float32),
            pltpu.VMEM((seq_len, width), low),
            pltpu.VMEM((seq_len, width), jnp.float32),
            exchange,
            exchange,
            exchange,
            exchange,
            pltpu.VMEM(expert_in.shape[1:], low),
            pltpu.VMEM(expert_out.shape[1:], low),
            pltpu.VMEM((experts_all // STAGES * slot_rows, expert_in.shape[2]), low),
            pltpu.VMEM((seq_len, width), jnp.float32),
            pltpu.SemaphoreType.DMA((4,)),
            pltpu.SemaphoreType.DMA((copies,)),
            pltpu.SemaphoreType.DMA((copies,)),
            pltpu.SemaphoreType.DMA((2,)),
            pltpu.SemaphoreType.DMA((2, STAGES)),
        ],
        compiler_params=pltpu.CompilerParams(
            collective_id=0, has_side_effects=True, vmem_limit_bytes=58 << 20
        ),
        name="encoder_layer",
    )(
        swap_list, tokens, expert_ids.reshape(1, seq_len), w_qkv, w_attn_out,
        gain_attn, gain_expert, router, capacity[None, :], expert_in, expert_out,
    )


def solution(mesh):
    return jax.shard_map(
        shards,
        mesh=mesh,
        in_specs=(
            P(("role", "dev"), None),
            P(("role", "dev"), None),
            P(("role", "dev"), None),
            P(("role", "dev"), None),
            P(),
            P(),
            P(),
            P(("role", "dev"), None, None),
            P(("role", "dev"), None, None),
            P(),
            P(),
        ),
        out_specs=P(("role", "dev"), None),
        check_vma=False,
    )
```
